128 devices in a mesh: section: 4 (over z), seq: 16 (over y, x), mp: 2 (over core).
Axes of the slice: x: 4, y: 4, z: 4, core: 2. Of those that a mesh axis runs over, the one named last changes fastest.
Arguments:
- fresh_input: bfloat16 [4, 8192, 2048], P('section', 'seq', 'mp'), may hold values from -6 to 6
- saved_input: bfloat16 [4, 8192, 2048], P('section', 'seq', 'mp'), may hold values from -6 to 6
- cotangent: bfloat16 [4, 8192, 2048], P('section', 'seq', 'mp'), may hold values from -4 to 4
- factor_one: bfloat16 [4, 32, 256, 256], P('section', 'seq'), may hold values from -0.375 to 0.375
- twiddle: bfloat16 [4, 256, 2048], P('section', None, 'mp'), may hold values from -4 to 4
- factor_two: bfloat16 [4, 256, 32, 32], P('section', 'seq'), may hold values from -1 to 1
- up_weight: bfloat16 [4, 4, 512, 2048], P('section', 'mp'), may hold values from -0.25 to 0.25
- down_weight: bfloat16 [4, 4, 2048, 512], P('section', 'mp'), may hold values from -0.125 to 0.125
Outputs:
- sent_activation: bfloat16 [4, 8192, 2048], P('section', 'seq', 'mp')
- sent_gradient: bfloat16 [4, 8192, 2048], P('section', 'seq', 'mp')
- up_gradient: float32 [4, 4, 512, 2048], P('section', 'mp', 'seq')
- down_gradient: float32 [4, 4, 2048, 512], P('section', 'mp', 'seq')
- twiddle_gradient: float32 [4, 256, 2048], P('section', 'seq', 'mp')
- first_gradient: float32 [4, 32, 256, 256], P('section', 'seq')
- second_gradient: float32 [4, 256, 32, 32], P('section', 'seq')
The draws below stay inside these ranges and needn't reach their ends.
All inputs are finite; a program needn't handle non-finite values.
Results may differ from the reference program's by a relative error of at most 0.01.
Values may be sent and summed in bfloat16 or wider, within the bound.
A program may use at most 128 MiB of HBM per device.

```python
import jax
import jax.numpy as jnp
from jax import lax

D = 2048
NBLK = 4
BS = 256
NB = 32
SEQ = 8192
DB = 512
FB = 2048
SECTIONS = 4
N_SECTION = 4


def steps_of(stream_key, shape, cuts, low, high):
    gain, own = 1.0, jax.random.fold_in(stream_key, 6)
    for dim, blocks in cuts:
        steps = jnp.exp(jax.random.uniform(jax.random.fold_in(own, dim), (blocks,), jnp.float32, low / len(cuts), high / len(cuts)))
        gain = gain * jnp.repeat(steps, shape[dim] // blocks).reshape([-1 if axis == dim else 1 for axis in range(len(shape))])
    return gain


def scatter_about(rng, dims, scale, limit, shards=(), dtype=jnp.bfloat16):
    values = scale * jax.random.normal(rng, dims, jnp.float32)
    if shards:
        values = values * steps_of(rng, dims, shards, -0.22, 0.18)
    return jnp.clip(values, -limit, limit).astype(dtype)


def setup_inputs(seed: int = 0) -> dict:
    streams_of = jax.random.split(jax.random.key(seed), 9)
    return {
        "fresh_input": scatter_about(streams_of[0], (SECTIONS, SEQ, D), 1.0, 6.0, ((0, 4), (1, 16), (2, 2))),
        "saved_input": scatter_about(streams_of[1], (SECTIONS, SEQ, D), 1.0, 6.0, ((0, 4), (1, 16), (2, 2))),
        "cotangent": scatter_about(streams_of[2], (SECTIONS, SEQ, D), 0.25, 4.0, ((0, 4), (1, 16), (2, 2))),
        "factor_one": scatter_about(streams_of[3], (SECTIONS, NB, BS, BS), BS ** -0.5, 0.375, ((0, 4), (1, 16))),
        "twiddle": scatter_about(streams_of[4], (SECTIONS, BS, D), 1.0, 4.0, ((0, 4), (2, 2))),
        "factor_two": scatter_about(streams_of[5], (SECTIONS, BS, NB, NB), NB ** -0.5, 1.0, ((0, 4), (1, 16))),
        "up_weight": scatter_about(streams_of[6], (SECTIONS, NBLK, DB, FB), DB ** -0.5, 0.25, ((0, 4), (1, 2))),
        "down_weight": scatter_about(streams_of[7], (SECTIONS, NBLK, FB, DB), FB ** -0.5, 0.125, ((0, 4), (1, 2))),
    }


def gelu_tanh(values):
    return jax.nn.gelu(values, approximate=True)

def mixer(inputs, factor_one, twiddle, factor_two):
    reshaped = inputs.astype(jnp.float32).reshape(NB, BS, D)
    inner = jnp.einsum('abk,akc->abc', factor_one.astype(jnp.float32), reshaped)
    twisted = (inner * twiddle.astype(jnp.float32)).astype(jnp.bfloat16)
    mixed = jnp.einsum('bij,jbc->ibc', factor_two.astype(jnp.float32), twisted.astype(jnp.float32)).astype(jnp.bfloat16)
    return (inner, twisted, mixed.reshape(SEQ, D))

def channel(inputs, mixed, up_weight, down_weight):
    gating = jax.nn.sigmoid(inputs.astype(jnp.float32))
    hidden = (inputs.astype(jnp.float32) + mixed.astype(jnp.float32) * gating).astype(jnp.bfloat16)
    lifted = jnp.einsum('tkd,kdf->tkf', hidden.reshape(SEQ, NBLK, DB).astype(jnp.float32), up_weight.astype(jnp.float32))
    activated = gelu_tanh(lifted).astype(jnp.bfloat16)
    projected = jnp.einsum('tkf,kfd->tkd', activated.astype(jnp.float32), down_weight.astype(jnp.float32))
    result = (hidden.astype(jnp.float32) + projected.reshape(SEQ, D)).astype(jnp.bfloat16)
    return (gating, hidden, lifted, activated, result)

def backward(inputs, incoming, factor_one, twiddle, factor_two, up_weight, down_weight):
    inner, twisted, mixed = mixer(inputs, factor_one, twiddle, factor_two)
    gating, hidden, lifted, activated, result = channel(inputs, mixed, up_weight, down_weight)
    up_f = up_weight.astype(jnp.float32)
    down_f = down_weight.astype(jnp.float32)
    incoming_blocks = incoming.astype(jnp.float32).reshape(SEQ, NBLK, DB)
    back_act = jnp.einsum('tkd,kfd->tkf', incoming_blocks, down_f)
    d_lifted = jax.vjp(gelu_tanh, lifted)[1](back_act)[0].astype(jnp.bfloat16)
    down_grad = jnp.einsum('tkf,tkd->kfd', activated.astype(jnp.float32), incoming_blocks)
    up_grad = jnp.einsum('tkd,tkf->kdf', hidden.astype(jnp.float32).reshape(SEQ, NBLK, DB), d_lifted.astype(jnp.float32))
    d_hidden = incoming.astype(jnp.float32) + jnp.einsum('tkf,kdf->tkd', d_lifted.astype(jnp.float32), up_f).reshape(SEQ, D)
    d_mixed = (d_hidden * gating).astype(jnp.bfloat16).reshape(NB, BS, D)
    second_grad = jnp.einsum('ibc,jbc->bij', d_mixed.astype(jnp.float32), twisted.astype(jnp.float32))
    d_twisted = jnp.einsum('bij,ibc->jbc', factor_two.astype(jnp.float32), d_mixed.astype(jnp.float32)).astype(jnp.bfloat16)
    twiddle_grad = lax.optimization_barrier(jnp.sum(d_twisted.astype(jnp.float32) * inner, axis=0))
    d_inner = (d_twisted.astype(jnp.float32) * twiddle.astype(jnp.float32)).astype(jnp.bfloat16)
    reshaped = inputs.astype(jnp.float32).reshape(NB, BS, D)
    first_grad = jnp.einsum('abc,akc->abk', d_inner.astype(jnp.float32), reshaped)
    local_back = jnp.einsum('abk,abc->akc', factor_one.astype(jnp.float32), d_inner.astype(jnp.float32)).reshape(SEQ, D)
    direct = d_hidden * (1.0 + mixed.astype(jnp.float32) * gating * (1.0 - gating))
    d_input = (direct + local_back).astype(jnp.bfloat16)
    return (d_input, up_grad, down_grad, twiddle_grad, first_grad, second_grad)

def reference(fresh_input, saved_input, cotangent, factor_one, twiddle, factor_two, up_weight, down_weight):
    outputs = []
    d_inputs = []
    up_list = []
    down_list = []
    twiddle_list = []
    first_list = []
    second_list = []
    for section in range(N_SECTION):
        mixed = mixer(fresh_input[section], factor_one[section], twiddle[section], factor_two[section])[2]
        outputs.append(channel(fresh_input[section], mixed, up_weight[section], down_weight[section])[4])
        pieces = backward(saved_input[section], cotangent[section], factor_one[section], twiddle[section], factor_two[section], up_weight[section], down_weight[section])
        d_inputs.append(pieces[0])
        up_list.append(pieces[1])
        down_list.append(pieces[2])
        twiddle_list.append(pieces[3])
        first_list.append(pieces[4])
        second_list.append(pieces[5])
    zeros_rows = jnp.zeros((SEQ, D), jnp.bfloat16)
    sent_activation = jnp.stack([zeros_rows] + outputs[:-1])
    sent_gradient = jnp.stack(d_inputs[1:] + [zeros_rows])
    return (sent_activation, sent_gradient, jnp.stack(up_list), jnp.stack(down_list), jnp.stack(twiddle_list), jnp.stack(first_list), jnp.stack(second_list))
```

```python
import functools
import math

import jax
import jax.numpy as jnp
from jax import lax
from jax.experimental import pallas as pl
from jax.experimental.pallas import tpu as pltpu
from jax.sharding import PartitionSpec as P

MESH = pl.DeviceIdType.MESH
BF = jnp.bfloat16
F32 = jnp.float32
C0 = math.sqrt(2.0 / math.pi)
C1 = 0.044715

NQ = 16
NS = 4
TOK = 512
HALF = 512
FB = 2048
GRP = 2


def nn(a, b):
    return jnp.dot(a, b, preferred_element_type=F32)


def nt(a, b):
    return lax.dot_general(a, b, (((1,), (1,)), ((), ())), preferred_element_type=F32)


def tn(a, b):
    return lax.dot_general(a, b, (((0,), (0,)), ((), ())), preferred_element_type=F32)


def iota(shape, dim):
    return lax.broadcasted_iota(jnp.int32, shape, dim)


def split(x):
    high = x.astype(BF)
    return high, (x - high.astype(F32)).astype(BF)


def kernel(
    vf_h, vs_h, g_h, f1_h, tw_h, f2_h, up_h, dn_h,
    oact, ograd, oup, odn, otw, ofirst, osecond,
    vs, vf, gg, f1, tw16, f2, up, dn, wmat,
    pin_s, pin_f, pdm, pmx_s, pmx_f, pdi,
    cin_s, cin_f, cdm, cmx_s, cmx_f, cdi,
    twc, hid, direct, act, dl, dh,
    part_up, part_dn, ra_up, ra_dn, rb_up, rb_dn,
    gsum, fg, fg_r, sg, sg_r, outf, dinp, zero, upo, dno, twg, sgo,
    ld, a2s, a2r, rss, rsr, zs, zr, mps, mpr, osem,
):
    sec = lax.axis_index("section")
    me = lax.axis_index("seq")
    core = lax.axis_index("mp")
    y, x = me // 4, me % 4

    def load(src, dst, i):
        copy = pltpu.make_async_copy(src, dst, ld.at[i])
        copy.start()
        return copy

    cols = [pl.ds(0, HALF), pl.ds(HALF, HALF)]
    l_f1 = load(f1_h, f1, 0)
    l_vs = [load(vs_h.at[:, cols[k]], vs.at[k], 1 + k) for k in range(2)]
    l_f2 = load(f2_h, f2, 3)
    own16 = pl.ds(pl.multiple_of(me * 16, 16), 16)
    l_tw = [load(tw_h.at[own16, cols[k]], tw16.at[k], 4 + k) for k in range(2)]
    l_vf = [load(vf_h.at[:, cols[k]], vf.at[k], 6 + k) for k in range(2)]
    l_g = [load(g_h.at[:, cols[k]], gg.at[k], 8 + k) for k in range(2)]
    l_up = [load(up_h.at[k], up.at[k], 10 + k) for k in range(2)]
    l_dn = [load(dn_h.at[k], dn.at[k], 12 + k) for k in range(2)]

    barrier = pltpu.get_barrier_semaphore()

    def peer(d):
        return ((y + d // 4) % 4) * 4 + (x + d % 4) % 4

    def greet(d, carry):
        pl.semaphore_signal(barrier, inc=1, device_id={"seq": peer(d)}, device_id_type=MESH)
        return carry

    lax.fori_loop(1, NQ, greet, 0)
    for by in (1, 3):
        pl.semaphore_signal(
            barrier, inc=1, device_id={"section": (sec + by) % 4}, device_id_type=MESH
        )
    pl.semaphore_signal(barrier, inc=1, device_id={"mp": 1 - core}, device_id_type=MESH)

    def own_rows(ref, k, q):
        return ref.at[k, :, pl.ds(pl.multiple_of(q * 16, 16), 16), :]

    def own_blocks(ref, k, q):
        return ref.at[k, pl.ds(q * 2, 2)]

    def exchange(src_of, dst_of, src, dst, st, k):
        i = 2 * st + k

        def one(d, carry):
            q = peer(d)
            pltpu.make_async_remote_copy(
                src_ref=src_of(src, k, q),
                dst_ref=dst_of(dst, k, me),
                send_sem=a2s.at[i],
                recv_sem=a2r.at[i],
                device_id={"seq": q},
                device_id_type=MESH,
            ).start()
            return carry

        lax.fori_loop(1, NQ, one, 0)
        pltpu.make_async_copy(src_of(src, k, me), dst_of(dst, k, me), a2r.at[i]).start()

    def arrived(dst, st, k):
        pltpu.make_async_copy(dst.at[k], dst.at[k], a2r.at[2 * st + k]).wait()

    def to_columns(src, dst, st, k):
        exchange(own_rows, own_blocks, src, dst, st, k)

    def to_positions(src, dst, st, k):
        exchange(own_blocks, own_rows, src, dst, st, k)

    def first_factor(v, dst, k):
        for a in range(2):
            dst[k, a] = nn(f1[a], v[k, pl.ds(256 * a, 256), :]).astype(BF)

    l_f1.wait()
    l_vs[0].wait()
    first_factor(vs, pin_s, 0)
    pl.semaphore_wait(barrier, NQ + 2)
    to_columns(pin_s, cin_s, 0, 0)
    l_vs[1].wait()
    first_factor(vs, pin_s, 1)
    to_columns(pin_s, cin_s, 0, 1)
    for k in range(2):
        l_vf[k].wait()
        first_factor(vf, pin_f, k)
        to_columns(pin_f, cin_f, 1, k)

    l_f2.wait()
    rows, lanes = iota((512, 512), 0), iota((512, 512), 1)
    swap = jnp.where(lanes == (rows % 16) * 32 + rows // 16, 1.0, 0.0).astype(BF)
    spread = jnp.where(iota((32, 512), 1) // 16 == iota((32, 512), 0), 1.0, 0.0).astype(BF)
    ordered = nn(swap, f2[...]).astype(BF)
    wide = nn(ordered, spread)
    wmat[...] = jnp.where(rows % 16 == lanes % 16, wide, 0.0).astype(BF)
    for k in range(2):
        l_tw[k].wait()

    def twisted(cin, k):
        return (cin[k].astype(F32) * tw16[k].astype(F32)[None]).astype(BF)

    for k in range(2):
        arrived(cin_s, 0, k)
        columns = twisted(cin_s, k)
        twc[k] = columns
        cmx_s[k] = nn(wmat[...], columns.reshape(512, HALF)).astype(BF).reshape(32, 16, HALF)
        to_positions(cmx_s, pmx_s, 2, k)
    for k in range(2):
        arrived(cin_f, 1, k)
        columns = twisted(cin_f, k)
        cmx_f[k] = nn(wmat[...], columns.reshape(512, HALF)).astype(BF).reshape(32, 16, HALF)
        to_positions(cmx_f, pmx_f, 3, k)

    def rs_parts(axis, part, ra, rb):
        mine = x if axis == "x" else y
        other = y if axis == "x" else x
        rows_half = part.shape[2] // 2

        def device(first, by):
            along = (first + by) % 4
            if axis == "x":
                return (y * 4 + along, along * 4 + x)
            return (along * 4 + x, y * 4 + along)

        def piece(phase, by, h):
            if phase == 0:
                return part.at[(mine + by) % 4, pl.ds(2 * h, 2)]
            return part.at[mine, (other + by) % 4, pl.ds(rows_half * h, rows_half)]

        def target(phase, by):
            return device(mine if phase == 0 else other, by)[phase]

        def land(phase, slot):
            return (ra if phase == 0 else rb).at[slot]

        return piece, target, land

    units = []
    for k in range(2):
        units.append(rs_parts("x", part_up.at[k], ra_up.at[k], rb_up.at[k]))
        units.append(rs_parts("y", part_dn.at[k], ra_dn.at[k], rb_dn.at[k]))

    def rs_copy(u, phase, slot, by, h, to):
        piece, target, land = units[u]
        return pltpu.make_async_remote_copy(
            src_ref=piece(phase, by, h),
            dst_ref=land(phase, slot),
            send_sem=rss.at[u, phase * 6 + slot],
            recv_sem=rsr.at[u, phase * 6 + slot],
            device_id={"seq": target(phase, to)},
            device_id_type=MESH,
        )

    SLOTS = ((2, 0, 1), (1, 1, 1), (2, 1, 3), (3, 0, 3), (1, 0, 1), (3, 1, 3))

    def rs_first(u, phase):
        for slot in (0, 2, 1, 3):
            rs_copy(u, phase, slot, *SLOTS[slot]).start()

    def rs_second(u, phase):
        piece, target, land = units[u]
        for slot, after in ((4, 0), (5, 2)):
            by, h, to = SLOTS[slot]
            rs_copy(u, phase, after, *SLOTS[after]).wait_recv()
            ref = piece(phase, by, h)
            ref[...] = (ref[...].astype(F32) + land(phase, after)[...].astype(F32)).astype(BF)
            rs_copy(u, phase, slot, by, h, to).start()

    def rs_third(u, phase, finish):
        piece, target, land = units[u]
        for h, left, right in ((0, 3, 4), (1, 1, 5)):
            for slot in (left, right):
                rs_copy(u, phase, slot, *SLOTS[slot]).wait_recv()
            ref = piece(phase, 0, h)
            total = (
                ref[...].astype(F32)
                + land(phase, left)[...].astype(F32)
                + land(phase, right)[...].astype(F32)
            )
            finish(ref, h, total)

    def keep(ref, h, total):
        ref[...] = total.astype(BF)

    def rs_sent(u):
        for phase in range(2):
            for slot in range(6):
                rs_copy(u, phase, slot, *SLOTS[slot]).wait_send()

    def gated(v, mixed, k, r):
        rs = pl.ds(r * 128, 128)
        values = v[k, rs, :].astype(F32)
        gate = jax.nn.sigmoid(values)
        mix = mixed[k, r // 2, pl.ds(pl.multiple_of((r % 2) * 128, 128), 128), :].astype(F32)
        return rs, values, gate, mix

    def chunk(j):
        return pl.ds(pl.multiple_of(j * 512, 512), 512)

    def channel_saved(k):
        def start(r, carry):
            rs, values, gate, mix = gated(vs, pmx_s, k, r)
            hid[k, rs, :] = (values + mix * gate).astype(BF)
            dh[rs, :] = gg[k, rs, :].astype(F32)
            return carry

        lax.fori_loop(0, 4, start, 0)

        def step(j, carry):
            up_part = up[k, :, chunk(j)]
            u = nn(hid[k], up_part)
            back = nt(gg[k], dn[k, chunk(j), :])
            square = u * u
            th = jnp.tanh(C0 * u * (1.0 + C1 * square))
            lift = 0.5 * (1.0 + th)
            act[j] = (u * lift).astype(BF)
            slope = lift + (0.5 * C0) * u * (1.0 - th * th) * (1.0 + (3.0 * C1) * square)
            d_lift = (back * slope).astype(BF)
            dl[j] = d_lift
            dh[...] += nt(d_lift, up_part)
            return carry

        lax.fori_loop(0, 4, step, 0)

        def end(r, carry):
            rs, values, gate, mix = gated(vs, pmx_s, k, r)
            d_hidden = dh[rs, :]
            pdm[k, r // 2, pl.ds(pl.multiple_of((r % 2) * 128, 128), 128), :] = (
                d_hidden * gate
            ).astype(BF)
            direct[k, rs, :] = d_hidden * (1.0 + mix * gate * (1.0 - gate))
            return carry

        lax.fori_loop(0, 4, end, 0)

    def gradients(k):
        def step_up(j, carry):
            total = tn(hid[k], dl[j]).astype(BF).reshape(4, 4, 32, 512)
            for yy in range(4):
                part_up[k, :, yy, :, chunk(j)] = total[yy]
            return carry

        lax.fori_loop(0, 4, step_up, 0)
        rs_first(2 * k, 0)

        def step_down(j, carry):
            part_dn[k, j] = tn(act[j], gg[k]).astype(BF).reshape(4, 128, 512)
            return carry

        lax.fori_loop(0, 4, step_down, 0)
        rs_first(2 * k + 1, 0)

    for k in range(2):
        l_g[k].wait()
        l_up[k].wait()
        l_dn[k].wait()
        arrived(pmx_s, 2, k)
        channel_saved(k)
        to_columns(pdm, cdm, 4, k)
        gradients(k)

    def columns_back(k):
        arrived(cdm, 4, k)
        grads = cdm[k].reshape(512, HALF)
        d_twisted = tn(wmat[...], grads).astype(BF).astype(F32).reshape(32, 16, HALF)
        cdi[k] = (d_twisted * tw16[k].astype(F32)[None]).astype(BF)
        to_positions(cdi, pdi, 5, k)
        twg[:, cols[k]] = jnp.sum(d_twisted * cin_s[k].astype(F32), axis=0)
        product = nt(grads, twc[k].reshape(512, HALF))
        if k == 0:
            gsum[...] = product
        else:
            gsum[...] += product

    columns_back(0)
    rs_second(0, 0)
    rs_second(1, 0)
    columns_back(1)
    rs_second(2, 0)
    rs_second(3, 0)

    rows2, lanes2 = iota((512, 512), 0), iota((512, 512), 1)
    picked = jnp.where(rows2 % 16 == lanes2 % 16, gsum[...], 0.0)
    gather = jnp.where(iota((512, 32), 0) // 16 == iota((512, 32), 1), 1.0, 0.0).astype(BF)
    high, low = split(picked)
    small = nn(high, gather) + nn(low, gather)
    back_swap = jnp.where(lanes2 == (rows2 % 32) * 16 + rows2 // 32, 1.0, 0.0).astype(BF)
    high, low = split(small)
    sg[...] = nn(back_swap, high) + nn(back_swap, low)

    def mp_copy(src, dst, i):
        return pltpu.make_async_remote_copy(
            src_ref=src,
            dst_ref=dst,
            send_sem=mps.at[i],
            recv_sem=mpr.at[i],
            device_id={"mp": 1 - core},
            device_id_type=MESH,
        )

    mp_copy(sg, sg_r, 0).start()

    def act_copy(k):
        return pltpu.make_async_remote_copy(
            src_ref=outf.at[k],
            dst_ref=oact.at[:, cols[k]],
            send_sem=zs.at[k],
            recv_sem=zr.at[k],
            device_id={"section": (sec + 1) % 4},
            device_id_type=MESH,
        )

    def grad_copy(k):
        return pltpu.make_async_remote_copy(
            src_ref=dinp.at[k],
            dst_ref=ograd.at[:, cols[k]],
            send_sem=zs.at[2 + k],
            recv_sem=zr.at[2 + k],
            device_id={"section": (sec + 3) % 4},
            device_id_type=MESH,
        )

    def channel_fresh(k):
        def start(r, carry):
            rs, values, gate, mix = gated(vf, pmx_f, k, r)
            hidden = (values + mix * gate).astype(BF)
            pmx_f[k, r // 2, pl.ds(pl.multiple_of((r % 2) * 128, 128), 128), :] = hidden
            dh[rs, :] = hidden.astype(F32)
            return carry

        lax.fori_loop(0, 4, start, 0)

        def step(j, carry):
            u = nn(pmx_f[k].reshape(TOK, HALF), up[k, :, chunk(j)])
            th = jnp.tanh(C0 * u * (1.0 + C1 * (u * u)))
            dh[...] += nn((0.5 * u * (1.0 + th)).astype(BF), dn[k, chunk(j), :])
            return carry

        lax.fori_loop(0, 4, step, 0)
        outf[k] = dh[...].astype(BF)

    zero[...] = jnp.zeros_like(zero)

    def blank(dst, k, i):
        return pltpu.make_async_copy(zero, dst.at[:, cols[k]], osem.at[i])

    @pl.when(sec == 0)
    def _():
        for k in range(2):
            blank(oact, k, k).start()

    @pl.when(sec == NS - 1)
    def _():
        for k in range(2):
            blank(ograd, k, k).start()

    for k in range(2):
        arrived(pmx_f, 3, k)
        channel_fresh(k)

        @pl.when(sec < NS - 1)
        def _():
            act_copy(k).start()

        rs_third(2 * k, 0, keep)
        rs_first(2 * k, 1)
        rs_third(2 * k + 1, 0, keep)
        rs_first(2 * k + 1, 1)

    for k in range(2):
        arrived(pdi, 5, k)
        for a in range(2):
            rs = pl.ds(256 * a, 256)
            dinp[k, rs, :] = (direct[k, rs, :] + tn(f1[a], pdi[k, a])).astype(BF)

        @pl.when(sec > 0)
        def _():
            grad_copy(k).start()

        for a in range(2):
            product = nt(pdi[k, a], vs[k, pl.ds(256 * a, 256), :])
            if k == 0:
                fg[a] = product
            else:
                fg[a] += product
    mp_copy(fg, fg_r, 1).start()

    def store(src, dst, i):
        copy = pltpu.make_async_copy(src, dst, osem.at[i])
        copy.start()
        return copy

    stores = [store(twg, otw, 2)]
    mp_copy(sg, sg_r, 0).wait()
    sgo[...] = sg[...] + sg_r[...]
    stores.append(store(sgo, osecond, 3))
    for u in range(4):
        rs_second(u, 1)
    mp_copy(fg, fg_r, 1).wait()
    fg[...] += fg_r[...]
    stores.append(store(fg, ofirst, 4))
    for u in range(4):
        k = u // 2
        out = (upo, dno)[u % 2]
        height = out.shape[1] // 2

        def last(ref, h, total):
            out[k, pl.ds(height * h, height), :] = total

        rs_third(u, 1, last)
        stores.append(store(out.at[k], (oup, odn)[u % 2].at[k], 5 + u))

    for st, (src, kind) in enumerate(
        ((pin_s, 0), (pin_f, 0), (cmx_s, 1), (cmx_f, 1), (pdm, 0), (cdi, 1))
    ):
        for k in range(2):
            ref = src.at[k, :, pl.ds(0, 240), :] if kind == 0 else src.at[k, pl.ds(0, 30)]
            pltpu.make_async_copy(ref, ref, a2s.at[2 * st + k]).wait()
    for u in range(4):
        rs_sent(u)

    @pl.when(sec < NS - 1)
    def _():
        for k in range(2):
            act_copy(k).wait_send()
            grad_copy(k).wait_recv()

    @pl.when(sec > 0)
    def _():
        for k in range(2):
            grad_copy(k).wait_send()
            act_copy(k).wait_recv()

    @pl.when(sec == 0)
    def _():
        for k in range(2):
            blank(oact, k, k).wait()

    @pl.when(sec == NS - 1)
    def _():
        for k in range(2):
            blank(ograd, k, k).wait()

    for copy in stores:
        copy.wait()


def body(fresh, saved, cotangent, factor_one, twiddle, factor_two, up_weight, down_weight):
    any_space = pl.BlockSpec(memory_space=pl.ANY)
    position = pltpu.VMEM((2, 2, 256, HALF), BF)
    column = pltpu.VMEM((2, 32, 16, HALF), BF)
    rows = pltpu.VMEM((2, TOK, HALF), BF)
    dma = pltpu.SemaphoreType.DMA
    outs = pl.pallas_call(
        kernel,
        out_shape=(
            jax.ShapeDtypeStruct((TOK, 1024), BF),
            jax.ShapeDtypeStruct((TOK, 1024), BF),
            jax.ShapeDtypeStruct((2, 32, FB), F32),
            jax.ShapeDtypeStruct((2, 128, 512), F32),
            jax.ShapeDtypeStruct((16, 1024), F32),
            jax.ShapeDtypeStruct((2, 256, 256), F32),
            jax.ShapeDtypeStruct((512, 32), F32),
        ),
        in_specs=[any_space] * 8,
        out_specs=(any_space,) * 7,
        scratch_shapes=[
            rows, rows, rows,
            pltpu.VMEM((2, 256, 256), BF),
            pltpu.VMEM((2, 16, HALF), BF),
            pltpu.VMEM((512, 32), BF),
            pltpu.VMEM((2, 512, FB), BF),
            pltpu.VMEM((2, FB, 512), BF),
            pltpu.VMEM((512, 512), BF),
            position, position, position, position, position, position,
            column, column, column, column, column, column,
            column,
            rows,
            pltpu.VMEM((2, TOK, HALF), F32),
            pltpu.VMEM((4, TOK, 512), BF),
            pltpu.VMEM((4, TOK, 512), BF),
            pltpu.VMEM((TOK, HALF), F32),
            pltpu.VMEM((2, 4, 4, 32, FB), BF),
            pltpu.VMEM((2, 4, 4, 128, 512), BF),
            pltpu.VMEM((2, 6, 2, 32, FB), BF),
            pltpu.VMEM((2, 6, 2, 128, 512), BF),
            pltpu.VMEM((2, 6, 16, FB), BF),
            pltpu.VMEM((2, 6, 64, 512), BF),
            pltpu.VMEM((512, 512), F32),
            pltpu.VMEM((2, 256, 256), F32),
            pltpu.VMEM((2, 256, 256), F32),
            pltpu.VMEM((512, 32), F32),
            pltpu.VMEM((512, 32), F32),
            rows, rows,
            pltpu.VMEM((TOK, HALF), BF),
            pltpu.VMEM((2, 32, FB), F32),
            pltpu.VMEM((2, 128, 512), F32),
            pltpu.VMEM((16, 1024), F32),
            pltpu.VMEM((512, 32), F32),
            dma((14,)), dma((12,)), dma((12,)), dma((4, 12)), dma((4, 12)),
            dma((4,)), dma((4,)), dma((2,)), dma((2,)), dma((9,)),
        ],
        compiler_params=pltpu.CompilerParams(
            collective_id=0, has_side_effects=True, vmem_limit_bytes=63 * 1024 * 1024
        ),
    )(
        fresh[0], saved[0], cotangent[0], factor_one[0], twiddle[0],
        factor_two[0].reshape(512, 32), up_weight[0], down_weight[0],
    )
    act, grad, up_grad, down_grad, twiddle_grad, first_grad, second_grad = outs
    return (
        act[None],
        grad[None],
        up_grad[None],
        down_grad[None],
        twiddle_grad[None],
        first_grad[None],
        second_grad.reshape(1, 16, 32, 32),
    )


def solution(mesh):
    return jax.shard_map(
        body,
        mesh=mesh,
        in_specs=(
            P("section", "seq", "mp"),
            P("section", "seq", "mp"),
            P("section", "seq", "mp"),
            P("section", "seq", None, None),
            P("section", None, "mp"),
            P("section", "seq", None, None),
            P("section", "mp", None, None),
            P("section", "mp", None, None),
        ),
        out_specs=(
            P("section", "seq", "mp"),
            P("section", "seq", "mp"),
            P("section", "mp", "seq", None),
            P("section", "mp", "seq", None),
            P("section", "seq", "mp"),
            P("section", "seq", None, None),
            P("section", "seq", None, None),
        ),
        check_vma=False,
    )
```

```python
import math

import jax
import jax.numpy as jnp
from jax import lax
from jax.experimental import pallas as pl
from jax.experimental.pallas import tpu as pltpu
from jax.sharding import PartitionSpec as P

MESH = pl.DeviceIdType.MESH
BF = jnp.bfloat16
F32 = jnp.float32
C0 = math.sqrt(2.0 / math.pi)
C1 = 0.044715

NQ = 16
NS = 4
TOK = 512
HALF = 512
FB = 2048
GRP = 2


def nn(a, b):
    return jnp.dot(a, b, preferred_element_type=F32)


def nt(a, b):
    return lax.dot_general(a, b, (((1,), (1,)), ((), ())), preferred_element_type=F32)


def tn(a, b):
    return lax.dot_general(a, b, (((0,), (0,)), ((), ())), preferred_element_type=F32)


def iota(shape, dim):
    return lax.broadcasted_iota(jnp.int32, shape, dim)


def split(x):
    high = x.astype(BF)
    return high, (x - high.astype(F32)).astype(BF)


def kernel(
    vf_h, vs_h, g_h, f1_h, tw_h, f2_h, up_h, dn_h,
    oact, ograd, oup, odn, otw, ofirst, osecond,
    vs, vf, gg, f1, tw16, tws, f2o, f2c, up, dn, wup, wdn, wmf, wms,
    pin_s, pin_f, pdi, pdr, pmx_f,
    ci, cv, cg, cdi, cdr, cin_f, cmx_f,
    twc, mix, dm, hid, act, dl, dh,
    part, mpb, ra, xsum, wgr,
    fg, fg_r, sgp, sgr, sg, outf, dinp, zero, upo, dno, twg, sgo,
    ld, a2s, a2r, nbs, nbr, rss, rsr, mxs, mxr, xss, xsr, zs, zr, sms, smr, osem,
):
    sec = lax.axis_index("section")
    me = lax.axis_index("seq")
    core = lax.axis_index("mp")
    y, x = me // 4, me % 4
    ks = x % 2
    kc = x // 2
    home = core == kc
    away = core != kc
    base = 64 * y + 32 * core

    def at16(start, size=16):
        return pl.ds(pl.multiple_of(start, 16), size)

    def wide(start):
        return pl.ds(pl.multiple_of(start, 512), 512)

    def load(src, dst, i):
        copy = pltpu.make_async_copy(src, dst, ld.at[i])
        copy.start()
        return copy

    cols = [pl.ds(0, HALF), pl.ds(HALF, HALF)]
    l_f1 = load(f1_h, f1, 0)
    l_vs = [load(vs_h.at[:, :, cols[k]], vs.at[k], 1 + k) for k in range(2)]
    l_g = [load(g_h.at[:, :, cols[k]], gg.at[k], 3 + k) for k in range(2)]
    l_f2 = load(f2_h, f2o, 5)
    l_tw = [load(tw_h.at[at16(me * 16), cols[k]], tw16.at[k], 6 + k) for k in range(2)]
    l_vf = [load(vf_h.at[:, :, cols[k]], vf.at[k], 8 + k) for k in range(2)]
    l_up = [load(up_h.at[k], up.at[k], 10 + k) for k in range(2)]
    l_dn = [load(dn_h.at[k], dn.at[k], 12 + k) for k in range(2)]

    barrier = pltpu.get_barrier_semaphore()

    def peer(d):
        return ((y + d // 4) % 4) * 4 + (x + d % 4) % 4

    def greet(d, carry):
        pl.semaphore_signal(
            barrier,
            inc=1,
            device_id={"seq": peer(d % 16), "mp": (core + d // 16) % 2},
            device_id_type=MESH,
        )
        return carry

    lax.fori_loop(1, 2 * NQ, greet, 0)
    for by in (1, 3):
        pl.semaphore_signal(
            barrier, inc=1, device_id={"section": (sec + by) % 4}, device_id_type=MESH
        )

    def remote(src, dst, send_sem, recv_sem, device):
        return pltpu.make_async_remote_copy(
            src_ref=src,
            dst_ref=dst,
            send_sem=send_sem,
            recv_sem=recv_sem,
            device_id=device,
            device_id_type=MESH,
        )

    def column_piece(src, dst, i, h, d):
        yy = (y + d // 4) % 4
        slot = (x + (d // 2) % 2) % 2
        cc = (core + d % 2) % 2
        return (
            src.at[slot, :, at16(64 * yy + 32 * cc + 16 * h), :],
            dst.at[h, pl.ds(2 * me, 2)],
            {"seq": yy * 4 + 2 * core + slot, "mp": cc},
        )

    def position_piece(src, dst, i, h, d):
        q = peer(d)
        return (
            src.at[h, pl.ds(2 * q, 2)],
            dst.at[ks, :, at16(base + 16 * h), :],
            {"seq": q, "mp": kc},
        )

    def scatter(piece, src, dst, i, h):
        def one(d, carry):
            a, b, device = piece(src, dst, i, h, d)
            remote(a, b, a2s.at[i], a2r.at[i], device).start()
            return carry

        lax.fori_loop(1, NQ, one, 0)
        a, b, device = piece(src, dst, i, h, 0)

        @pl.when(home)
        def _():
            pltpu.make_async_copy(a, b, a2r.at[i]).start()

        @pl.when(away)
        def _():
            remote(a, b, a2s.at[i], a2r.at[i], device).start()

    def fresh_columns(k, q):
        return (
            pin_f.at[k, :, at16(q * 16), :],
            cin_f.at[k, pl.ds(me * 2, 2)],
        )

    def fresh_positions(k, q):
        return (
            cmx_f.at[k, pl.ds(q * 2, 2)],
            pmx_f.at[k, :, at16(me * 16), :],
        )

    def fresh(piece, i, k):
        def one(d, carry):
            q = peer(d)
            remote(*piece(k, q), a2s.at[i], a2r.at[i], {"seq": q}).start()
            return carry

        lax.fori_loop(1, NQ, one, 0)
        a, b = piece(k, me)
        pltpu.make_async_copy(a, b, a2r.at[i]).start()

    def arrived(ref, i):
        pltpu.make_async_copy(ref, ref, a2r.at[i]).wait()

    def first_factor(v, dst, k):
        for a in range(2):
            dst[k, a] = nn(f1[a], v[k, a]).astype(BF)

    l_f1.wait()
    for k in range(2):
        l_vs[k].wait()
        first_factor(vs, pin_s, k)
    for k in range(2):
        l_g[k].wait()
    pl.semaphore_wait(barrier, 2 * NQ + 1)

    scatter(column_piece, pin_s, ci, 0, 0)
    scatter(column_piece, vs, cv, 2, 0)
    scatter(column_piece, gg, cg, 4, 0)

    def fact_copy(by):
        return remote(
            f2_h, f2c.at[ks], nbs.at[by - 1], nbr.at[ks], {"seq": y * 4 + (x + by) % 4}
        )

    def tw_rows(c):
        return tw_h.at[at16(64 * y + 32 * c, 32), wide(512 * ks)]

    partner = {"mp": 1 - core}

    def lent():
        return (
            remote(tw_rows(1 - core), tws, nbs.at[3], nbr.at[2], partner),
            remote(up_h.at[ks], wup, nbs.at[4], nbr.at[3], partner),
            remote(dn_h.at[ks], wdn, nbs.at[5], nbr.at[4], partner),
        )

    @pl.when(home)
    def _():
        pltpu.make_async_copy(f2_h, f2c.at[ks], nbr.at[ks]).start()
        for by in range(1, 4):
            fact_copy(by).start()
        for copy in lent():
            copy.start()
        pltpu.make_async_copy(tw_rows(core), tws, nbr.at[2]).start()
        pltpu.make_async_copy(up_h.at[ks], wup, nbr.at[3]).start()
        pltpu.make_async_copy(dn_h.at[ks], wdn, nbr.at[4]).start()

    scatter(column_piece, pin_s, ci, 1, 1)
    scatter(column_piece, vs, cv, 3, 1)
    scatter(column_piece, gg, cg, 5, 1)

    for k in range(2):
        l_vf[k].wait()
        first_factor(vf, pin_f, k)
        fresh(fresh_columns, 10 + k, k)

    def block_diagonal(f2):
        rows, lanes = iota((512, 512), 0), iota((512, 512), 1)
        swap = jnp.where(lanes == (rows % 16) * 32 + rows // 16, 1.0, 0.0).astype(BF)
        spread = jnp.where(iota((32, 512), 1) // 16 == iota((32, 512), 0), 1.0, 0.0).astype(BF)
        ordered = nn(swap, f2).astype(BF)
        return jnp.where(rows % 16 == lanes % 16, nn(ordered, spread), 0.0).astype(BF)

    def near(ref, i):
        pltpu.make_async_copy(ref, ref, nbr.at[i]).wait()

    l_f2.wait()
    wmf[...] = block_diagonal(f2o[...])
    for h in range(2):
        near(f2c.at[h], h)
        wms[h] = block_diagonal(f2c[h])
    near(tws, 2)
    for k in range(2):
        l_tw[k].wait()

    def small_copy(h, cc):
        return remote(
            sgp.at[h],
            sgr.at[x],
            sms.at[2 * h + cc],
            smr.at[x],
            {"seq": y * 4 + 2 * core + h, "mp": cc},
        )

    def twiddle_copy(h):
        return remote(
            twg.at[h],
            otw.at[:, wide(512 * ks)],
            sms.at[4 + h],
            smr.at[4 + ks],
            {"seq": y * 4 + 2 * core + h, "mp": kc},
        )

    def small_each(h, is_self, is_other):
        here = 2 * core + h == x
        for cc in range(2):
            same = jnp.logical_and(here, core == cc)

            if is_self:

                @pl.when(same)
                def _():
                    is_self(pltpu.make_async_copy(sgp.at[h], sgr.at[x], smr.at[x]))

            @pl.when(jnp.logical_not(same))
            def _():
                is_other(small_copy(h, cc))

        same = jnp.logical_and(here, home)

        if is_self:

            @pl.when(same)
            def _():
                is_self(
                    pltpu.make_async_copy(
                        twg.at[h], otw.at[:, wide(512 * ks)], smr.at[4 + ks]
                    )
                )

        @pl.when(jnp.logical_not(same))
        def _():
            is_other(twiddle_copy(h))

    def chunk(j):
        return pl.ds(pl.multiple_of(j * 512, 512), 512)

    def saved(h):
        tw = tws[pl.ds(16 * h, 16), :].astype(F32)[None]
        arrived(ci.at[h], h)
        columns = (ci[h].astype(F32) * tw).astype(BF)
        twc[h] = columns
        mix[...] = nn(wms[h], columns.reshape(512, HALF)).astype(BF).reshape(32, 16, HALF)
        arrived(cv.at[h], 2 + h)
        arrived(cg.at[h], 4 + h)
        top = 512 * h

        def gated(r):
            blocks = pl.ds(r * 8, 8)
            values = cv[h, blocks].reshape(128, HALF).astype(F32)
            mixed = mix[blocks].reshape(128, HALF).astype(F32)
            return blocks, values, jax.nn.sigmoid(values), mixed

        def start(r, carry):
            blocks, values, gate, mixed = gated(r)
            hid[pl.ds(pl.multiple_of(top + r * 128, 128), 128), :] = (
                values + mixed * gate
            ).astype(BF)
            dh[pl.ds(pl.multiple_of(r * 128, 128), 128), :] = (
                cg[h, blocks].reshape(128, HALF).astype(F32)
            )
            return carry

        lax.fori_loop(0, 4, start, 0)
        if h == 0:
            near(wup, 3)
            near(wdn, 4)

        def step(j, carry):
            up_part = wup[:, chunk(j)]
            u = nn(hid[pl.ds(top, 512), :], up_part)
            back = nt(cg[h].reshape(512, HALF), wdn[chunk(j), :])
            square = u * u
            th = jnp.tanh(C0 * u * (1.0 + C1 * square))
            lift = 0.5 * (1.0 + th)
            act[j, pl.ds(top, 512), :] = (u * lift).astype(BF)
            slope = lift + (0.5 * C0) * u * (1.0 - th * th) * (1.0 + (3.0 * C1) * square)
            d_lift = (back * slope).astype(BF)
            dl[j, pl.ds(top, 512), :] = d_lift
            dh[...] += nt(d_lift, up_part)
            return carry

        lax.fori_loop(0, 4, step, 0)

        def end(r, carry):
            blocks, values, gate, mixed = gated(r)
            rs = pl.ds(pl.multiple_of(r * 128, 128), 128)
            d_hidden = dh[rs, :]
            dm[rs, :] = (d_hidden * gate).astype(BF)
            cdr[h, blocks] = (
                (d_hidden * (1.0 + mixed * gate * (1.0 - gate))).astype(BF).reshape(8, 16, HALF)
            )
            return carry

        lax.fori_loop(0, 4, end, 0)
        scatter(position_piece, cdr, pdr, 8 + h, h)
        d_twisted = tn(wms[h], dm[...]).astype(BF).astype(F32).reshape(32, 16, HALF)
        cdi[h] = (d_twisted * tw).astype(BF)
        scatter(position_piece, cdi, pdi, 6 + h, h)
        twg[h] = jnp.sum(d_twisted * ci[h].astype(F32), axis=0)

        rows, lanes = iota((512, 512), 0), iota((512, 512), 1)
        product = nt(dm[...], twc[h].reshape(512, HALF))
        high, low = split(jnp.where(rows % 16 == lanes % 16, product, 0.0))
        packed = jnp.zeros((128, 128), F32)
        for group in range(4):
            gather = jnp.where(
                iota((512, 128), 1) == 32 * group + iota((512, 128), 0) // 16, 1.0, 0.0
            ).astype(BF)
            some = slice(128 * group, 128 * group + 128)
            packed = packed + nn(high[some], gather) + nn(low[some], gather)
        sgp[h] = packed
        small_each(h, lambda copy: copy.start(), lambda copy: copy.start())

    for h in range(2):
        saved(h)

    for k in range(2):
        arrived(cin_f.at[k], 10 + k)
        columns = (cin_f[k].astype(F32) * tw16[k].astype(F32)[None]).astype(BF)
        cmx_f[k] = nn(wmf[...], columns.reshape(512, HALF)).astype(BF).reshape(32, 16, HALF)
        fresh(fresh_positions, 12 + k, k)

    def step_up(j, carry):
        total = tn(hid[...], dl[j]).astype(BF).reshape(4, 4, 32, 512)
        part[0, :, :, pl.ds(pl.multiple_of(j * 32, 32), 32), :] = total
        return carry

    lax.fori_loop(0, 4, step_up, 0)

    def step_down(j, carry):
        part[1, j] = tn(act[j], cg[...].reshape(1024, HALF)).astype(BF).reshape(4, 128, 512)
        return carry

    lax.fori_loop(0, 4, step_down, 0)

    def core_copy(t):
        return remote(
            part.at[1 - core, (y + t) % 4], mpb.at[t], mxs.at[t], mxr.at[t], partner
        )

    ORDER = (2, 1, 3, 0)
    for t in ORDER:
        core_copy(t).start()

    SLOTS = ((2, 0, 1), (1, 1, 1), (2, 1, 3), (3, 0, 3), (1, 0, 1), (3, 1, 3))

    def piece(by, h):
        return part.at[core, (y + by) % 4, pl.ds(2 * h, 2)]

    def rs_copy(slot):
        by, h, to = SLOTS[slot]
        return remote(
            piece(by, h),
            ra.at[slot],
            rss.at[slot],
            rsr.at[slot],
            {"seq": ((y + to) % 4) * 4 + x},
        )

    def both(t):
        core_copy(t).wait_recv()
        ref = part.at[core, (y + t) % 4]
        ref[...] = (ref[...].astype(F32) + mpb[t].astype(F32)).astype(BF)

    both(2)
    rs_copy(0).start()
    rs_copy(2).start()
    both(1)
    rs_copy(1).start()
    both(3)
    rs_copy(3).start()
    both(0)

    def rs_second():
        for slot, after in ((4, 0), (5, 2)):
            by, h, to = SLOTS[slot]
            rs_copy(after).wait_recv()
            ref = piece(by, h)
            ref[...] = (ref[...].astype(F32) + ra[after].astype(F32)).astype(BF)
            rs_copy(slot).start()

    def spread_copy(xx):
        return remote(
            xsum.at[xx],
            wgr.at[core, ks],
            xss.at[xx],
            xsr.at[core, ks],
            {"seq": y * 4 + xx, "mp": kc},
        )

    def spread_each(xx, is_self, is_other):
        same = jnp.logical_and(x == xx, home)

        if is_self:

            @pl.when(same)
            def _():
                is_self(
                    pltpu.make_async_copy(xsum.at[xx], wgr.at[core, ks], xsr.at[core, ks])
                )

        @pl.when(jnp.logical_not(same))
        def _():
            is_other(spread_copy(xx))

    def rs_third():
        for h, left, right in ((0, 3, 4), (1, 1, 5)):
            for slot in (left, right):
                rs_copy(slot).wait_recv()
            xsum[pl.ds(2 * h, 2)] = (
                piece(0, h)[...].astype(F32) + ra[left].astype(F32) + ra[right].astype(F32)
            ).astype(BF)
            for xx in (2 * h, 2 * h + 1):
                spread_each(xx, lambda copy: copy.start(), lambda copy: copy.start())

    def act_copy(k):
        return remote(
            outf.at[k],
            oact.at[:, cols[k]],
            zs.at[k],
            zr.at[k],
            {"section": (sec + 1) % 4},
        )

    def grad_copy(k):
        return remote(
            dinp.at[k],
            ograd.at[:, cols[k]],
            zs.at[2 + k],
            zr.at[2 + k],
            {"section": (sec + 3) % 4},
        )

    def channel_fresh(k):
        def start(r, carry):
            rs = pl.ds(pl.multiple_of((r % 2) * 128, 128), 128)
            values = vf[k, r // 2, rs, :].astype(F32)
            mixed = pmx_f[k, r // 2, rs, :].astype(F32)
            hidden = (values + mixed * jax.nn.sigmoid(values)).astype(BF)
            pmx_f[k, r // 2, rs, :] = hidden
            dh[pl.ds(pl.multiple_of(r * 128, 128), 128), :] = hidden.astype(F32)
            return carry

        lax.fori_loop(0, 4, start, 0)

        def step(j, carry):
            u = nn(pmx_f[k].reshape(TOK, HALF), up[k, :, chunk(j)])
            th = jnp.tanh(C0 * u * (1.0 + C1 * (u * u)))
            dh[...] += nn((0.5 * u * (1.0 + th)).astype(BF), dn[k, chunk(j), :])
            return carry

        lax.fori_loop(0, 4, step, 0)
        outf[k] = dh[...].astype(BF)

    zero[...] = jnp.zeros_like(zero)

    def blank(dst, k, i):
        return pltpu.make_async_copy(zero, dst.at[:, cols[k]], osem.at[i])

    @pl.when(sec == 0)
    def _():
        for k in range(2):
            blank(oact, k, k).start()

    @pl.when(sec == NS - 1)
    def _():
        for k in range(2):
            blank(ograd, k, k).start()

    for k in range(2):
        l_up[k].wait()
        l_dn[k].wait()
        arrived(pmx_f.at[k], 12 + k)
        channel_fresh(k)

        @pl.when(sec < NS - 1)
        def _():
            act_copy(k).start()

        if k == 0:
            rs_second()

    for h in range(2):
        arrived(pdr.at[0], 8 + h)
        arrived(pdi.at[0], 6 + h)
    for k in range(2):
        for a in range(2):
            dinp[k, pl.ds(256 * a, 256), :] = (
                pdr[k, a].astype(F32) + tn(f1[a], pdi[k, a])
            ).astype(BF)

        @pl.when(sec > 0)
        def _():
            grad_copy(k).start()

    rs_third()
    for a in range(2):
        fg[a] = nt(pdi[0, a], vs[0, a]) + nt(pdi[1, a], vs[1, a])
    first_copy = remote(fg, fg_r, mxs.at[4], mxr.at[4], partner)
    first_copy.start()

    def store(src, dst, i):
        copy = pltpu.make_async_copy(src, dst, osem.at[i])
        copy.start()
        return copy

    for k in range(4):
        pltpu.make_async_copy(sgr.at[k], sgr.at[k], smr.at[k]).wait()
    packed = (sgr[0] + sgr[1]) + (sgr[2] + sgr[3])
    high, low = split(packed)
    for group in range(4):
        pick = jnp.where(iota((128, 32), 0) == 32 * group + iota((128, 32), 1), 1.0, 0.0).astype(
            BF
        )
        sg[pl.ds(128 * group, 128), :] = nn(high, pick) + nn(low, pick)
    rows, lanes = iota((512, 512), 0), iota((512, 512), 1)
    back_swap = jnp.where(lanes == (rows % 32) * 16 + rows // 32, 1.0, 0.0).astype(BF)
    high, low = split(sg[...])
    sgo[...] = nn(back_swap, high) + nn(back_swap, low)
    stores = [store(sgo, osecond, 2)]
    first_copy.wait()
    fg[...] += fg_r[...]
    stores.append(store(fg, ofirst, 3))
    for slot in range(2):
        for kind in range(2):
            pltpu.make_async_copy(
                wgr.at[kind, slot], wgr.at[kind, slot], xsr.at[kind, slot]
            ).wait()
        for j in range(4):
            upo[slot, :, pl.ds(512 * j, 512)] = wgr[0, slot, pl.ds(32 * j, 32), :].astype(F32)
        dno[slot] = wgr[1, slot].astype(F32)
        stores.append(store(upo.at[slot], oup.at[slot], 4 + slot))
        stores.append(store(dno.at[slot], odn.at[slot], 6 + slot))

    sent = ((pin_s, 0, 0), (vs, 2, 0), (gg, 4, 0), (cdi, 6, 1), (cdr, 8, 1), (pin_f, 10, 0), (cmx_f, 12, 1))
    for src, i, kind in sent:
        for k in range(2):
            most = src.at[k, :, pl.ds(0, 240), :] if kind == 0 else src.at[k, pl.ds(0, 30)]
            pltpu.make_async_copy(most, most, a2s.at[i + k]).wait()
            if i < 10:
                rest = src.at[k, :, pl.ds(0, 16), :] if kind == 0 else src.at[k, pl.ds(0, 2)]

                @pl.when(away)
                def _():
                    pltpu.make_async_copy(rest, rest, a2s.at[i + k]).wait()

    @pl.when(home)
    def _():
        for by in range(1, 4):
            fact_copy(by).wait_send()
        for copy in lent():
            copy.wait_send()

    for h in range(2):
        small_each(h, None, lambda copy: copy.wait_send())
    for slot in range(2):
        otw_part = otw.at[:, cols[slot]]
        pltpu.make_async_copy(otw_part, otw_part, smr.at[4 + slot]).wait()
    for t in range(4):
        core_copy(t).wait_send()
    for slot in range(6):
        rs_copy(slot).wait_send()
    for xx in range(4):
        spread_each(xx, None, lambda copy: copy.wait_send())

    @pl.when(sec < NS - 1)
    def _():
        for k in range(2):
            act_copy(k).wait_send()
            grad_copy(k).wait_recv()

    @pl.when(sec > 0)
    def _():
        for k in range(2):
            grad_copy(k).wait_send()
            act_copy(k).wait_recv()

    @pl.when(sec == 0)
    def _():
        for k in range(2):
            blank(oact, k, k).wait()

    @pl.when(sec == NS - 1)
    def _():
        for k in range(2):
            blank(ograd, k, k).wait()

    for copy in stores:
        copy.wait()


def hand_on(*refs):
    count = (len(refs) - 1) // 3
    sems = refs[-1]
    into = [
        pltpu.make_async_copy(refs[i], refs[2 * count + i], sems.at[0, i]) for i in range(count)
    ]
    out = [
        pltpu.make_async_copy(refs[2 * count + i], refs[count + i], sems.at[1, i])
        for i in range(count)
    ]
    for copy in into:
        copy.start()
    for i in range(count):
        into[i].wait()
        out[i].start()
    for copy in out:
        copy.wait()


def body(fresh, saved, cotangent, factor_one, twiddle, factor_two, up_weight, down_weight):
    any_space = pl.BlockSpec(memory_space=pl.ANY)
    position = pltpu.VMEM((2, 2, 256, HALF), BF)
    column = pltpu.VMEM((2, 32, 16, HALF), BF)
    rows = pltpu.VMEM((2, TOK, HALF), BF)
    square = pltpu.VMEM((512, 512), BF)
    fact = pltpu.VMEM((512, 32), BF)
    dma = pltpu.SemaphoreType.DMA
    shapes = (
        jax.ShapeDtypeStruct((TOK, 1024), BF),
        jax.ShapeDtypeStruct((TOK, 1024), BF),
        jax.ShapeDtypeStruct((2, 32, FB), F32),
        jax.ShapeDtypeStruct((2, 128, 512), F32),
        jax.ShapeDtypeStruct((16, 1024), F32),
        jax.ShapeDtypeStruct((2, 256, 256), F32),
        jax.ShapeDtypeStruct((512, 32), F32),
    )
    outs = pl.pallas_call(
        kernel,
        out_shape=shapes,
        in_specs=[any_space] * 8,
        out_specs=(any_space,) * 7,
        scratch_shapes=[
            position, position, position,
            pltpu.VMEM((2, 256, 256), BF),
            pltpu.VMEM((2, 16, HALF), BF),
            pltpu.VMEM((32, HALF), BF),
            fact,
            pltpu.VMEM((2, 512, 32), BF),
            pltpu.VMEM((2, 512, FB), BF),
            pltpu.VMEM((2, FB, 512), BF),
            pltpu.VMEM((512, FB), BF),
            pltpu.VMEM((FB, 512), BF),
            square,
            pltpu.VMEM((2, 512, 512), BF),
            position, position, position, position, position,
            column, column, column, column, column, column, column,
            column,
            pltpu.VMEM((32, 16, HALF), BF),
            square,
            pltpu.VMEM((2 * TOK, HALF), BF),
            pltpu.VMEM((4, 2 * TOK, 512), BF),
            pltpu.VMEM((4, 2 * TOK, 512), BF),
            pltpu.VMEM((TOK, HALF), F32),
            pltpu.VMEM((2, 4, 4, 128, 512), BF),
            pltpu.VMEM((4, 4, 128, 512), BF),
            pltpu.VMEM((6, 2, 128, 512), BF),
            pltpu.VMEM((4, 128, 512), BF),
            pltpu.VMEM((2, 2, 128, 512), BF),
            pltpu.VMEM((2, 256, 256), F32),
            pltpu.VMEM((2, 256, 256), F32),
            pltpu.VMEM((2, 128, 128), F32),
            pltpu.VMEM((4, 128, 128), F32),
            pltpu.VMEM((512, 32), F32),
            rows, rows,
            pltpu.VMEM((TOK, HALF), BF),
            pltpu.VMEM((2, 32, FB), F32),
            pltpu.VMEM((2, 128, 512), F32),
            pltpu.VMEM((2, 16, HALF), F32),
            pltpu.VMEM((512, 32), F32),
            dma((14,)), dma((14,)), dma((14,)), dma((6,)), dma((5,)), dma((6,)), dma((6,)),
            dma((5,)), dma((5,)), dma((4,)), dma((2, 2)), dma((4,)), dma((4,)),
            dma((6,)), dma((6,)), dma((8,)),
        ],
        compiler_params=pltpu.CompilerParams(
            collective_id=0, has_side_effects=True, vmem_limit_bytes=63 * 1024 * 1024
        ),
    )(
        fresh.reshape(2, 256, 1024), saved.reshape(2, 256, 1024), cotangent.reshape(2, 256, 1024),
        factor_one[0], twiddle[0], factor_two[0].reshape(512, 32), up_weight[0], down_weight[0],
    )
    act, grad, up_grad, down_grad, twiddle_grad, first_grad, second_grad = pl.pallas_call(
        hand_on,
        out_shape=shapes,
        in_specs=[any_space] * 7,
        out_specs=(any_space,) * 7,
        scratch_shapes=[pltpu.VMEM(part.shape, part.dtype) for part in shapes] + [dma((2, 7))],
    )(*outs)
    return (
        act[None],
        grad[None],
        up_grad[None],
        down_grad[None],
        twiddle_grad[None],
        first_grad[None],
        second_grad.reshape(1, 16, 32, 32),
    )


def solution(mesh):
    return jax.shard_map(
        body,
        mesh=mesh,
        in_specs=(
            P("section", "seq", "mp"),
            P("section", "seq", "mp"),
            P("section", "seq", "mp"),
            P("section", "seq", None, None),
            P("section", None, "mp"),
            P("section", "seq", None, None),
            P("section", "mp", None, None),
            P("section", "mp", None, None),
        ),
        out_specs=(
            P("section", "seq", "mp"),
            P("section", "seq", "mp"),
            P("section", "mp", "seq", None),
            P("section", "mp", "seq", None),
            P("section", "seq", "mp"),
            P("section", "seq", None, None),
            P("section", "seq", None, None),
        ),
        check_vma=False,
    )
```

```python
import math

import jax
import jax.numpy as jnp
from jax import lax
from jax.experimental import pallas as pl
from jax.experimental.pallas import tpu as pltpu
from jax.sharding import PartitionSpec as P

MESH = pl.DeviceIdType.MESH
BF = jnp.bfloat16
F32 = jnp.float32
C0 = math.sqrt(2.0 / math.pi)
C1 = 0.044715

NQ = 16
NS = 4
TOK = 512
HALF = 512
FB = 2048
GRP = 2


def nn(a, b):
    return jnp.dot(a, b, preferred_element_type=F32)


def nt(a, b):
    return lax.dot_general(a, b, (((1,), (1,)), ((), ())), preferred_element_type=F32)


def tn(a, b):
    return lax.dot_general(a, b, (((0,), (0,)), ((), ())), preferred_element_type=F32)


def iota(shape, dim):
    return lax.broadcasted_iota(jnp.int32, shape, dim)


def split(x):
    high = x.astype(BF)
    return high, (x - high.astype(F32)).astype(BF)


def kernel(
    vf_h, vs_h, g_h, f1_h, tw_h, f2_h, up_h, dn_h,
    oact, ograd, oup, odn, otw, ofirst, osecond,
    vs, vf, gg, f1, tw16, tws, f2o, f2c, up, dn, wup, wdn, wmf, wms,
    pin_s, pin_f, pdi, pdr, pmx_f,
    ci, cv, cg, cdi, cdr, cin_f, cmx_f,
    twc, mix, dm, hid, act, dl, dh,
    part, mpb, ra, xsum, wgr,
    fg, fg_r, sgp, sgr, sg, outf, dinp, zero, upo, dno, twg, sgo,
    ld, a2s, a2r, nbs, nbr, rss, rsr, mxs, mxr, xss, xsr, zs, zr, sms, smr, osem,
):
    sec = lax.axis_index("section")
    me = lax.axis_index("seq")
    core = lax.axis_index("mp")
    y, x = me // 4, me % 4
    ks = x % 2
    kc = x // 2
    home = core == kc
    away = core != kc
    base = 64 * y + 32 * core

    def at16(start, size=16):
        return pl.ds(pl.multiple_of(start, 16), size)

    def wide(start):
        return pl.ds(pl.multiple_of(start, 512), 512)

    def load(src, dst, i):
        copy = pltpu.make_async_copy(src, dst, ld.at[i])
        copy.start()
        return copy

    cols = [pl.ds(0, HALF), pl.ds(HALF, HALF)]
    l_f1 = load(f1_h, f1, 0)
    l_vs = [load(vs_h.at[:, :, cols[k]], vs.at[k], 1 + k) for k in range(2)]
    l_g = [load(g_h.at[:, :, cols[k]], gg.at[k], 3 + k) for k in range(2)]
    l_f2 = load(f2_h, f2o, 5)
    l_tw = [load(tw_h.at[at16(me * 16), cols[k]], tw16.at[k], 6 + k) for k in range(2)]
    l_vf = [load(vf_h.at[:, :, cols[k]], vf.at[k], 8 + k) for k in range(2)]
    l_up = [load(up_h.at[k], up.at[k], 10 + k) for k in range(2)]
    l_dn = [load(dn_h.at[k], dn.at[k], 12 + k) for k in range(2)]

    barrier = pltpu.get_barrier_semaphore()

    def peer(d):
        return ((y + d // 4) % 4) * 4 + (x + d % 4) % 4

    def greet(d, carry):
        pl.semaphore_signal(
            barrier,
            inc=1,
            device_id={"seq": peer(d % 16), "mp": (core + d // 16) % 2},
            device_id_type=MESH,
        )
        return carry

    lax.fori_loop(1, 2 * NQ, greet, 0)
    for by in (1, 3):
        pl.semaphore_signal(
            barrier, inc=1, device_id={"section": (sec + by) % 4}, device_id_type=MESH
        )

    def remote(src, dst, send_sem, recv_sem, device):
        return pltpu.make_async_remote_copy(
            src_ref=src,
            dst_ref=dst,
            send_sem=send_sem,
            recv_sem=recv_sem,
            device_id=device,
            device_id_type=MESH,
        )

    def column_piece(src, dst, i, h, d):
        yy = (y + d // 4) % 4
        slot = (x + (d // 2) % 2) % 2
        cc = (core + d % 2) % 2
        return (
            src.at[slot, :, at16(64 * yy + 32 * cc + 16 * h), :],
            dst.at[h, pl.ds(2 * me, 2)],
            {"seq": yy * 4 + 2 * core + slot, "mp": cc},
        )

    def position_piece(src, dst, i, h, d):
        q = peer(d)
        return (
            src.at[h, 2 * q + i % 2],
            dst.at[ks, i % 2, at16(base + 16 * h), :],
            {"seq": q, "mp": kc},
        )

    def scatter(piece, src, dst, i, h):
        def one(d, carry):
            a, b, device = piece(src, dst, i, h, d)
            remote(a, b, a2s.at[i], a2r.at[i], device).start()
            return carry

        lax.fori_loop(1, NQ, one, 0)
        a, b, device = piece(src, dst, i, h, 0)

        @pl.when(home)
        def _():
            pltpu.make_async_copy(a, b, a2r.at[i]).start()

        @pl.when(away)
        def _():
            remote(a, b, a2s.at[i], a2r.at[i], device).start()

    def fresh_columns(k, q):
        return (
            pin_f.at[k, :, at16(q * 16), :],
            cin_f.at[k, pl.ds(me * 2, 2)],
        )

    def fresh_positions(k, q):
        return (
            cmx_f.at[k, pl.ds(q * 2, 2)],
            pmx_f.at[k, :, at16(me * 16), :],
        )

    def fresh(piece, i, k):
        def one(d, carry):
            q = peer(d)
            remote(*piece(k, q), a2s.at[i], a2r.at[i], {"seq": q}).start()
            return carry

        lax.fori_loop(1, NQ, one, 0)
        a, b = piece(k, me)
        pltpu.make_async_copy(a, b, a2r.at[i]).start()

    def arrived(ref, i):
        pltpu.make_async_copy(ref, ref, a2r.at[i]).wait()

    def first_factor(v, dst, k):
        for a in range(2):
            dst[k, a] = nn(f1[a], v[k, a]).astype(BF)

    def send_v(h):
        if h == 0:
            for k in range(2):
                l_vs[k].wait()
        scatter(column_piece, vs, cv, 2 + h, h)

    def send_g(h):
        if h == 0:
            for k in range(2):
                l_g[k].wait()
        scatter(column_piece, gg, cg, 4 + h, h)

    def send_inner(h):
        scatter(column_piece, pin_s, ci, h, h)

    def send_fresh(k):
        fresh(fresh_columns, 10 + k, k)

    def factor_saved():
        l_f1.wait()
        for k in range(2):
            first_factor(vs, pin_s, k)

    def factor_fresh(k):
        l_vf[k].wait()
        first_factor(vf, pin_f, k)

    def fact_copy(by):
        return remote(
            f2_h, f2c.at[ks], nbs.at[by - 1], nbr.at[ks], {"seq": y * 4 + (x + by) % 4}
        )

    def tw_rows(c):
        return tw_h.at[at16(64 * y + 32 * c, 32), wide(512 * ks)]

    partner = {"mp": 1 - core}

    def lent():
        return (
            remote(tw_rows(1 - core), tws, nbs.at[3], nbr.at[2], partner),
            remote(up_h.at[ks], wup, nbs.at[4], nbr.at[3], partner),
            remote(dn_h.at[ks], wdn, nbs.at[5], nbr.at[4], partner),
        )

    def lend():
        @pl.when(home)
        def _():
            pltpu.make_async_copy(f2_h, f2c.at[ks], nbr.at[ks]).start()
            for by in range(1, 4):
                fact_copy(by).start()
            for copy in lent():
                copy.start()
            pltpu.make_async_copy(tw_rows(core), tws, nbr.at[2]).start()
            pltpu.make_async_copy(up_h.at[ks], wup, nbr.at[3]).start()
            pltpu.make_async_copy(dn_h.at[ks], wdn, nbr.at[4]).start()

    def block_diagonal(f2):
        rows, lanes = iota((512, 512), 0), iota((512, 512), 1)
        swap = jnp.where(lanes == (rows % 16) * 32 + rows // 16, 1.0, 0.0).astype(BF)
        spread = jnp.where(iota((32, 512), 1) // 16 == iota((32, 512), 0), 1.0, 0.0).astype(BF)
        ordered = nn(swap, f2).astype(BF)
        return jnp.where(rows % 16 == lanes % 16, nn(ordered, spread), 0.0).astype(BF)

    def near(ref, i):
        pltpu.make_async_copy(ref, ref, nbr.at[i]).wait()

    def fact_fresh():
        l_f2.wait()
        wmf[...] = block_diagonal(f2o[...])
        for k in range(2):
            l_tw[k].wait()

    def fact_saved():
        for h in range(2):
            near(f2c.at[h], h)
            wms[h] = block_diagonal(f2c[h])
        near(tws, 2)

    def small_copy(h, cc):
        return remote(
            sgp.at[h],
            sgr.at[x],
            sms.at[2 * h + cc],
            smr.at[x],
            {"seq": y * 4 + 2 * core + h, "mp": cc},
        )

    def twiddle_copy(h):
        return remote(
            twg.at[h],
            otw.at[:, wide(512 * ks)],
            sms.at[4 + h],
            smr.at[4 + ks],
            {"seq": y * 4 + 2 * core + h, "mp": kc},
        )

    def small_each(h, is_self, is_other):
        here = 2 * core + h == x
        for cc in range(2):
            same = jnp.logical_and(here, core == cc)

            if is_self:

                @pl.when(same)
                def _():
                    is_self(pltpu.make_async_copy(sgp.at[h], sgr.at[x], smr.at[x]))

            @pl.when(jnp.logical_not(same))
            def _():
                is_other(small_copy(h, cc))

        same = jnp.logical_and(here, home)

        if is_self:

            @pl.when(same)
            def _():
                is_self(
                    pltpu.make_async_copy(
                        twg.at[h], otw.at[:, wide(512 * ks)], smr.at[4 + ks]
                    )
                )

        @pl.when(jnp.logical_not(same))
        def _():
            is_other(twiddle_copy(h))

    def chunk(j):
        return pl.ds(pl.multiple_of(j * 512, 512), 512)

    def saved(h, mid=None, after=None):
        tw = tws[pl.ds(16 * h, 16), :].astype(F32)[None]
        arrived(ci.at[h], h)
        columns = (ci[h].astype(F32) * tw).astype(BF)
        twc[h] = columns
        mix[...] = nn(wms[h], columns.reshape(512, HALF)).astype(BF).reshape(32, 16, HALF)
        if mid:
            mid()
        arrived(cv.at[h], 2 + h)
        arrived(cg.at[h], 4 + h)
        if after:
            after()
        top = 512 * h

        def gated(r):
            blocks = pl.ds(r * 8, 8)
            values = cv[h, blocks].reshape(128, HALF).astype(F32)
            mixed = mix[blocks].reshape(128, HALF).astype(F32)
            return blocks, values, jax.nn.sigmoid(values), mixed

        def start(r, carry):
            blocks, values, gate, mixed = gated(r)
            hid[pl.ds(pl.multiple_of(top + r * 128, 128), 128), :] = (
                values + mixed * gate
            ).astype(BF)
            dh[pl.ds(pl.multiple_of(r * 128, 128), 128), :] = (
                cg[h, blocks].reshape(128, HALF).astype(F32)
            )
            return carry

        lax.fori_loop(0, 4, start, 0)
        if h == 0:
            near(wup, 3)
            near(wdn, 4)

        def step(j, carry):
            up_part = wup[:, chunk(j)]
            u = nn(hid[pl.ds(top, 512), :], up_part)
            back = nt(cg[h].reshape(512, HALF), wdn[chunk(j), :])
            square = u * u
            th = jnp.tanh(C0 * u * (1.0 + C1 * square))
            lift = 0.5 * (1.0 + th)
            act[j, pl.ds(top, 512), :] = (u * lift).astype(BF)
            slope = lift + (0.5 * C0) * u * (1.0 - th * th) * (1.0 + (3.0 * C1) * square)
            d_lift = (back * slope).astype(BF)
            dl[j, pl.ds(top, 512), :] = d_lift
            dh[...] += nt(d_lift, up_part)
            return carry

        lax.fori_loop(0, 4, step, 0)

        def end(r, carry):
            blocks, values, gate, mixed = gated(r)
            rs = pl.ds(pl.multiple_of(r * 128, 128), 128)
            d_hidden = dh[rs, :]
            dm[rs, :] = (d_hidden * gate).astype(BF)
            cdr[h, blocks] = (
                (d_hidden * (1.0 + mixed * gate * (1.0 - gate))).astype(BF).reshape(8, 16, HALF)
            )
            return carry

        lax.fori_loop(0, 4, end, 0)
        d_twisted = tn(wms[h], dm[...]).astype(BF).astype(F32).reshape(32, 16, HALF)
        cdi[h] = (d_twisted * tw).astype(BF)
        for a in range(2):
            scatter(position_piece, cdi, pdi, 6 + a, h)
            scatter(position_piece, cdr, pdr, 8 + a, h)
        twg[h] = jnp.sum(d_twisted * ci[h].astype(F32), axis=0)

        rows, lanes = iota((512, 512), 0), iota((512, 512), 1)
        product = nt(dm[...], twc[h].reshape(512, HALF))
        high, low = split(jnp.where(rows % 16 == lanes % 16, product, 0.0))
        packed = jnp.zeros((128, 128), F32)
        for group in range(4):
            gather = jnp.where(
                iota((512, 128), 1) == 32 * group + iota((512, 128), 0) // 16, 1.0, 0.0
            ).astype(BF)
            some = slice(128 * group, 128 * group + 128)
            packed = packed + nn(high[some], gather) + nn(low[some], gather)
        sgp[h] = packed
        small_each(h, lambda copy: copy.start(), lambda copy: copy.start())

    def second_fresh(k):
        arrived(cin_f.at[k], 10 + k)
        columns = (cin_f[k].astype(F32) * tw16[k].astype(F32)[None]).astype(BF)
        cmx_f[k] = nn(wmf[...], columns.reshape(512, HALF)).astype(BF).reshape(32, 16, HALF)
        fresh(fresh_positions, 12 + k, k)

    def gradients():
        def step_up(j, carry):
            total = tn(hid[...], dl[j]).astype(BF).reshape(4, 4, 32, 512)
            part[0, :, :, pl.ds(pl.multiple_of(j * 32, 32), 32), :] = total
            return carry

        lax.fori_loop(0, 4, step_up, 0)

        def step_down(j, carry):
            part[1, j] = tn(act[j], cg[...].reshape(1024, HALF)).astype(BF).reshape(4, 128, 512)
            return carry

        lax.fori_loop(0, 4, step_down, 0)

        for t in ORDER:
            core_copy(t).start()

    ORDER = (2, 1, 3, 0)

    def core_copy(t):
        return remote(
            part.at[1 - core, (y + t) % 4], mpb.at[t], mxs.at[t], mxr.at[t], partner
        )

    SLOTS = ((2, 0, 1), (1, 1, 1), (2, 1, 3), (3, 0, 3), (1, 0, 1), (3, 1, 3))

    def piece(by, h):
        return part.at[core, (y + by) % 4, pl.ds(2 * h, 2)]

    def rs_copy(slot):
        by, h, to = SLOTS[slot]
        return remote(
            piece(by, h),
            ra.at[slot],
            rss.at[slot],
            rsr.at[slot],
            {"seq": ((y + to) % 4) * 4 + x},
        )

    def both(t):
        core_copy(t).wait_recv()
        ref = part.at[core, (y + t) % 4]
        ref[...] = (ref[...].astype(F32) + mpb[t].astype(F32)).astype(BF)

    def core_sums():
        for t in ORDER:
            both(t)

    def rs_first():
        for slot in (0, 2, 1, 3):
            rs_copy(slot).start()

    def rs_second():
        for slot, after in ((4, 0), (5, 2)):
            by, h, to = SLOTS[slot]
            rs_copy(after).wait_recv()
            ref = piece(by, h)
            ref[...] = (ref[...].astype(F32) + ra[after].astype(F32)).astype(BF)
            rs_copy(slot).start()

    def spread_copy(xx):
        return remote(
            xsum.at[xx],
            wgr.at[core, ks],
            xss.at[xx],
            xsr.at[core, ks],
            {"seq": y * 4 + xx, "mp": kc},
        )

    def spread_each(xx, is_self, is_other):
        same = jnp.logical_and(x == xx, home)

        if is_self:

            @pl.when(same)
            def _():
                is_self(
                    pltpu.make_async_copy(xsum.at[xx], wgr.at[core, ks], xsr.at[core, ks])
                )

        @pl.when(jnp.logical_not(same))
        def _():
            is_other(spread_copy(xx))

    def rs_third():
        for h, left, right in ((0, 3, 4), (1, 1, 5)):
            for slot in (left, right):
                rs_copy(slot).wait_recv()
            xsum[pl.ds(2 * h, 2)] = (
                piece(0, h)[...].astype(F32) + ra[left].astype(F32) + ra[right].astype(F32)
            ).astype(BF)
            for xx in (2 * h, 2 * h + 1):
                spread_each(xx, lambda copy: copy.start(), lambda copy: copy.start())

    def act_copy(k):
        return remote(
            outf.at[k],
            oact.at[:, cols[k]],
            zs.at[k],
            zr.at[k],
            {"section": (sec + 1) % 4},
        )

    def grad_copy(k, a):
        half = pl.ds(256 * a, 256)
        return remote(
            dinp.at[k, half],
            ograd.at[half, cols[k]],
            zs.at[2 + 2 * a + k],
            zr.at[2 + 2 * a + k],
            {"section": (sec + 3) % 4},
        )

    def channel_fresh(k):
        def start(r, carry):
            rs = pl.ds(pl.multiple_of((r % 2) * 128, 128), 128)
            values = vf[k, r // 2, rs, :].astype(F32)
            mixed = pmx_f[k, r // 2, rs, :].astype(F32)
            hidden = (values + mixed * jax.nn.sigmoid(values)).astype(BF)
            pmx_f[k, r // 2, rs, :] = hidden
            dh[pl.ds(pl.multiple_of(r * 128, 128), 128), :] = hidden.astype(F32)
            return carry

        lax.fori_loop(0, 4, start, 0)

        def step(j, carry):
            u = nn(pmx_f[k].reshape(TOK, HALF), up[k, :, chunk(j)])
            th = jnp.tanh(C0 * u * (1.0 + C1 * (u * u)))
            dh[...] += nn((0.5 * u * (1.0 + th)).astype(BF), dn[k, chunk(j), :])
            return carry

        lax.fori_loop(0, 4, step, 0)
        outf[k] = dh[...].astype(BF)

    zero[...] = jnp.zeros_like(zero)

    def blank(dst, k, i):
        return pltpu.make_async_copy(zero, dst.at[:, cols[k]], osem.at[i])

    @pl.when(sec == 0)
    def _():
        for k in range(2):
            blank(oact, k, k).start()

    @pl.when(sec == NS - 1)
    def _():
        for k in range(2):
            blank(ograd, k, k).start()

    def mix_fresh(k):
        l_up[k].wait()
        l_dn[k].wait()
        arrived(pmx_f.at[k], 12 + k)
        channel_fresh(k)

        @pl.when(sec < NS - 1)
        def _():
            act_copy(k).start()

    def finish_saved():
        for a in range(2):
            arrived(pdr.at[:, a], 8 + a)
            arrived(pdi.at[:, a], 6 + a)
            for k in range(2):
                dinp[k, pl.ds(256 * a, 256), :] = (
                    pdr[k, a].astype(F32) + tn(f1[a], pdi[k, a])
                ).astype(BF)

            @pl.when(sec > 0)
            def _():
                for k in range(2):
                    grad_copy(k, a).start()

    pl.semaphore_wait(barrier, 2 * NQ + 1)

    send_v(0)
    send_g(0)
    lend()
    factor_saved()
    send_inner(0)
    send_v(1)
    send_g(1)
    send_inner(1)
    factor_fresh(0)
    send_fresh(0)
    factor_fresh(1)
    send_fresh(1)
    fact_fresh()
    fact_saved()
    saved(0)
    second_fresh(0)
    second_fresh(1)
    saved(1)
    gradients()
    core_sums()
    rs_first()
    mix_fresh(0)
    finish_saved()
    rs_second()
    mix_fresh(1)
    rs_third()

    for a in range(2):
        fg[a] = nt(pdi[0, a], vs[0, a]) + nt(pdi[1, a], vs[1, a])
    first_copy = remote(fg, fg_r, mxs.at[4], mxr.at[4], partner)
    first_copy.start()

    def store(src, dst, i):
        copy = pltpu.make_async_copy(src, dst, osem.at[i])
        copy.start()
        return copy

    for k in range(4):
        pltpu.make_async_copy(sgr.at[k], sgr.at[k], smr.at[k]).wait()
    packed = (sgr[0] + sgr[1]) + (sgr[2] + sgr[3])
    high, low = split(packed)
    for group in range(4):
        pick = jnp.where(iota((128, 32), 0) == 32 * group + iota((128, 32), 1), 1.0, 0.0).astype(
            BF
        )
        sg[pl.ds(128 * group, 128), :] = nn(high, pick) + nn(low, pick)
    rows, lanes = iota((512, 512), 0), iota((512, 512), 1)
    back_swap = jnp.where(lanes == (rows % 32) * 16 + rows // 32, 1.0, 0.0).astype(BF)
    high, low = split(sg[...])
    sgo[...] = nn(back_swap, high) + nn(back_swap, low)
    stores = [store(sgo, osecond, 2)]
    first_copy.wait()
    fg[...] += fg_r[...]
    stores.append(store(fg, ofirst, 3))
    for slot in range(2):
        for kind in range(2):
            pltpu.make_async_copy(
                wgr.at[kind, slot], wgr.at[kind, slot], xsr.at[kind, slot]
            ).wait()
        for j in range(4):
            upo[slot, :, pl.ds(512 * j, 512)] = wgr[0, slot, pl.ds(32 * j, 32), :].astype(F32)
        dno[slot] = wgr[1, slot].astype(F32)
        stores.append(store(upo.at[slot], oup.at[slot], 4 + slot))
        stores.append(store(dno.at[slot], odn.at[slot], 6 + slot))

    sent = ((pin_s, 0, 0), (vs, 2, 0), (gg, 4, 0), (cdi, 6, 2), (cdr, 8, 2), (pin_f, 10, 0), (cmx_f, 12, 1))
    for src, i, kind in sent:
        for k in range(2):
            if kind == 0:
                most, rest = src.at[k, :, pl.ds(0, 240), :], src.at[k, :, pl.ds(0, 16), :]
            elif kind == 1:
                most, rest = src.at[k, pl.ds(0, 30)], None
            else:
                most, rest = src.at[:, pl.ds(0, 15)], src.at[:, pl.ds(0, 1)]
            pltpu.make_async_copy(most, most, a2s.at[i + k]).wait()
            if i < 10:

                @pl.when(away)
                def _():
                    pltpu.make_async_copy(rest, rest, a2s.at[i + k]).wait()

    @pl.when(home)
    def _():
        for by in range(1, 4):
            fact_copy(by).wait_send()
        for copy in lent():
            copy.wait_send()

    for h in range(2):
        small_each(h, None, lambda copy: copy.wait_send())
    for slot in range(2):
        otw_part = otw.at[:, cols[slot]]
        pltpu.make_async_copy(otw_part, otw_part, smr.at[4 + slot]).wait()
    for t in range(4):
        core_copy(t).wait_send()
    for slot in range(6):
        rs_copy(slot).wait_send()
    for xx in range(4):
        spread_each(xx, None, lambda copy: copy.wait_send())

    @pl.when(sec < NS - 1)
    def _():
        for k in range(2):
            act_copy(k).wait_send()
            for a in range(2):
                grad_copy(k, a).wait_recv()

    @pl.when(sec > 0)
    def _():
        for k in range(2):
            act_copy(k).wait_recv()
            for a in range(2):
                grad_copy(k, a).wait_send()

    @pl.when(sec == 0)
    def _():
        for k in range(2):
            blank(oact, k, k).wait()

    @pl.when(sec == NS - 1)
    def _():
        for k in range(2):
            blank(ograd, k, k).wait()

    for copy in stores:
        copy.wait()


def hand_on(*refs):
    count = (len(refs) - 1) // 3
    sems = refs[-1]
    into = [
        pltpu.make_async_copy(refs[i], refs[2 * count + i], sems.at[0, i]) for i in range(count)
    ]
    out = [
        pltpu.make_async_copy(refs[2 * count + i], refs[count + i], sems.at[1, i])
        for i in range(count)
    ]
    for copy in into:
        copy.start()
    for i in range(count):
        into[i].wait()
        out[i].start()
    for copy in out:
        copy.wait()


def body(fresh, saved, cotangent, factor_one, twiddle, factor_two, up_weight, down_weight):
    any_space = pl.BlockSpec(memory_space=pl.ANY)
    position = pltpu.VMEM((2, 2, 256, HALF), BF)
    column = pltpu.VMEM((2, 32, 16, HALF), BF)
    rows = pltpu.VMEM((2, TOK, HALF), BF)
    square = pltpu.VMEM((512, 512), BF)
    fact = pltpu.VMEM((512, 32), BF)
    dma = pltpu.SemaphoreType.DMA
    shapes = (
        jax.ShapeDtypeStruct((TOK, 1024), BF),
        jax.ShapeDtypeStruct((TOK, 1024), BF),
        jax.ShapeDtypeStruct((2, 32, FB), F32),
        jax.ShapeDtypeStruct((2, 128, 512), F32),
        jax.ShapeDtypeStruct((16, 1024), F32),
        jax.ShapeDtypeStruct((2, 256, 256), F32),
        jax.ShapeDtypeStruct((512, 32), F32),
    )
    outs = pl.pallas_call(
        kernel,
        out_shape=shapes,
        in_specs=[any_space] * 8,
        out_specs=(any_space,) * 7,
        scratch_shapes=[
            position, position, position,
            pltpu.VMEM((2, 256, 256), BF),
            pltpu.VMEM((2, 16, HALF), BF),
            pltpu.VMEM((32, HALF), BF),
            fact,
            pltpu.VMEM((2, 512, 32), BF),
            pltpu.VMEM((2, 512, FB), BF),
            pltpu.VMEM((2, FB, 512), BF),
            pltpu.VMEM((512, FB), BF),
            pltpu.VMEM((FB, 512), BF),
            square,
            pltpu.VMEM((2, 512, 512), BF),
            position, position, position, position, position,
            column, column, column, column, column, column, column,
            column,
            pltpu.VMEM((32, 16, HALF), BF),
            square,
            pltpu.VMEM((2 * TOK, HALF), BF),
            pltpu.VMEM((4, 2 * TOK, 512), BF),
            pltpu.VMEM((4, 2 * TOK, 512), BF),
            pltpu.VMEM((TOK, HALF), F32),
            pltpu.VMEM((2, 4, 4, 128, 512), BF),
            pltpu.VMEM((4, 4, 128, 512), BF),
            pltpu.VMEM((6, 2, 128, 512), BF),
            pltpu.VMEM((4, 128, 512), BF),
            pltpu.VMEM((2, 2, 128, 512), BF),
            pltpu.VMEM((2, 256, 256), F32),
            pltpu.VMEM((2, 256, 256), F32),
            pltpu.VMEM((2, 128, 128), F32),
            pltpu.VMEM((4, 128, 128), F32),
            pltpu.VMEM((512, 32), F32),
            rows, rows,
            pltpu.VMEM((TOK, HALF), BF),
            pltpu.VMEM((2, 32, FB), F32),
            pltpu.VMEM((2, 128, 512), F32),
            pltpu.VMEM((2, 16, HALF), F32),
            pltpu.VMEM((512, 32), F32),
            dma((14,)), dma((14,)), dma((14,)), dma((6,)), dma((5,)), dma((6,)), dma((6,)),
            dma((5,)), dma((5,)), dma((4,)), dma((2, 2)), dma((6,)), dma((6,)),
            dma((6,)), dma((6,)), dma((8,)),
        ],
        compiler_params=pltpu.CompilerParams(
            collective_id=0, has_side_effects=True, vmem_limit_bytes=63 * 1024 * 1024
        ),
    )(
        fresh.reshape(2, 256, 1024), saved.reshape(2, 256, 1024), cotangent.reshape(2, 256, 1024),
        factor_one[0], twiddle[0], factor_two[0].reshape(512, 32), up_weight[0], down_weight[0],
    )
    act, grad, up_grad, down_grad, twiddle_grad, first_grad, second_grad = pl.pallas_call(
        hand_on,
        out_shape=shapes,
        in_specs=[any_space] * 7,
        out_specs=(any_space,) * 7,
        scratch_shapes=[pltpu.VMEM(part.shape, part.dtype) for part in shapes] + [dma((2, 7))],
    )(*outs)
    return (
        act[None],
        grad[None],
        up_grad[None],
        down_grad[None],
        twiddle_grad[None],
        first_grad[None],
        second_grad.reshape(1, 16, 32, 32),
    )


def solution(mesh):
    return jax.shard_map(
        body,
        mesh=mesh,
        in_specs=(
            P("section", "seq", "mp"),
            P("section", "seq", "mp"),
            P("section", "seq", "mp"),
            P("section", "seq", None, None),
            P("section", None, "mp"),
            P("section", "seq", None, None),
            P("section", "mp", None, None),
            P("section", "mp", None, None),
        ),
        out_specs=(
            P("section", "seq", "mp"),
            P("section", "seq", "mp"),
            P("section", "mp", "seq", None),
            P("section", "mp", "seq", None),
            P("section", "seq", "mp"),
            P("section", "seq", None, None),
            P("section", "seq", None, None),
        ),
        check_vma=False,
    )
```

```python
import math

import jax
import jax.numpy as jnp
from jax import lax
from jax.experimental import pallas as pl
from jax.experimental.pallas import tpu as pltpu
from jax.sharding import PartitionSpec as P

MESH = pl.DeviceIdType.MESH
BF = jnp.bfloat16
F32 = jnp.float32
C0 = math.sqrt(2.0 / math.pi)
C1 = 0.044715

NQ = 16
NS = 4
TOK = 512
HALF = 512
FB = 2048
GRP = 2


def nn(a, b):
    return jnp.dot(a, b, preferred_element_type=F32)


def nt(a, b):
    return lax.dot_general(a, b, (((1,), (1,)), ((), ())), preferred_element_type=F32)


def tn(a, b):
    return lax.dot_general(a, b, (((0,), (0,)), ((), ())), preferred_element_type=F32)


def iota(shape, dim):
    return lax.broadcasted_iota(jnp.int32, shape, dim)


def split(x):
    high = x.astype(BF)
    return high, (x - high.astype(F32)).astype(BF)


def kernel(
    vf_h, vs_h, g_h, f1_h, tw_h, f2_h, up_h, dn_h,
    oact, ograd, oup, odn, otw, ofirst, osecond,
    vs, vf, gg, f1, tw16, tws, f2o, f2c, up, dn, wup, wdn, wmf, wms,
    pin_s, pin_f, pdi, pdr, pmx_f,
    ci, cv, cg, cdi, cdr, cin_f, cmx_f,
    twc, mix, dm, hid, act, dl, dh,
    part, mpb, ra, xsum, wgr,
    fg, fg_r, sgp, sgr, sg, outf, dinp, zero, upo, dno, twg, sgo,
    ld, a2s, a2r, nbs, nbr, rss, rsr, mxs, mxr, xss, xsr, zs, zr, sms, smr, osem,
):
    sec = lax.axis_index("section")
    me = lax.axis_index("seq")
    core = lax.axis_index("mp")
    y, x = me // 4, me % 4
    ks = x % 2
    kc = x // 2
    home = core == kc
    away = core != kc
    base = 64 * y + 32 * core

    def at16(start, size=16):
        return pl.ds(pl.multiple_of(start, 16), size)

    def wide(start):
        return pl.ds(pl.multiple_of(start, 512), 512)

    def load(src, dst, i):
        copy = pltpu.make_async_copy(src, dst, ld.at[i])
        copy.start()
        return copy

    cols = [pl.ds(0, HALF), pl.ds(HALF, HALF)]
    l_f1 = load(f1_h, f1, 0)
    l_vs = [load(vs_h.at[:, :, cols[k]], vs.at[k], 1 + k) for k in range(2)]
    l_g = [load(g_h.at[:, :, cols[k]], gg.at[k], 3 + k) for k in range(2)]
    l_f2 = load(f2_h, f2o, 5)
    l_tw = [load(tw_h.at[at16(me * 16), cols[k]], tw16.at[k], 6 + k) for k in range(2)]
    l_vf = [load(vf_h.at[:, :, cols[k]], vf.at[k], 8 + k) for k in range(2)]
    l_up = [load(up_h.at[k], up.at[k], 10 + k) for k in range(2)]
    l_dn = [load(dn_h.at[k], dn.at[k], 12 + k) for k in range(2)]

    barrier = pltpu.get_barrier_semaphore()

    def peer(d):
        return ((y + d // 4) % 4) * 4 + (x + d % 4) % 4

    def greet(d, carry):
        pl.semaphore_signal(
            barrier,
            inc=1,
            device_id={"seq": peer(d % 16), "mp": (core + d // 16) % 2},
            device_id_type=MESH,
        )
        return carry

    lax.fori_loop(1, 2 * NQ, greet, 0)
    for by in (1, 3):
        pl.semaphore_signal(
            barrier, inc=1, device_id={"section": (sec + by) % 4}, device_id_type=MESH
        )

    def remote(src, dst, send_sem, recv_sem, device):
        return pltpu.make_async_remote_copy(
            src_ref=src,
            dst_ref=dst,
            send_sem=send_sem,
            recv_sem=recv_sem,
            device_id=device,
            device_id_type=MESH,
        )

    def column_piece(src, dst, i, h, d):
        yy = (y + d // 4) % 4
        slot = (x + (d // 2) % 2) % 2
        cc = (core + d % 2) % 2
        return (
            src.at[slot, :, at16(64 * yy + 32 * cc + 16 * h), :],
            dst.at[h, pl.ds(2 * me, 2)],
            {"seq": yy * 4 + 2 * core + slot, "mp": cc},
        )

    def position_piece(src, dst, i, h, d):
        q = peer(d)
        return (
            src.at[h, 2 * q + i % 2],
            dst.at[ks, i % 2, at16(base + 16 * h), :],
            {"seq": q, "mp": kc},
        )

    def scatter(piece, src, dst, i, h):
        def one(d, carry):
            a, b, device = piece(src, dst, i, h, d)
            remote(a, b, a2s.at[i], a2r.at[i], device).start()
            return carry

        lax.fori_loop(1, NQ, one, 0)
        a, b, device = piece(src, dst, i, h, 0)

        @pl.when(home)
        def _():
            pltpu.make_async_copy(a, b, a2r.at[i]).start()

        @pl.when(away)
        def _():
            remote(a, b, a2s.at[i], a2r.at[i], device).start()

    def fresh_columns(k, q):
        return (
            pin_f.at[k, :, at16(q * 16), :],
            cin_f.at[k, pl.ds(me * 2, 2)],
        )

    def fresh_positions(k, q):
        return (
            cmx_f.at[k, pl.ds(q * 2, 2)],
            pmx_f.at[k, :, at16(me * 16), :],
        )

    def fresh(piece, i, k):
        def one(d, carry):
            q = peer(d)
            remote(*piece(k, q), a2s.at[i], a2r.at[i], {"seq": q}).start()
            return carry

        lax.fori_loop(1, NQ, one, 0)
        a, b = piece(k, me)
        pltpu.make_async_copy(a, b, a2r.at[i]).start()

    def arrived(ref, i):
        pltpu.make_async_copy(ref, ref, a2r.at[i]).wait()

    def first_factor(v, dst, k):
        for a in range(2):
            dst[k, a] = nn(f1[a], v[k, a]).astype(BF)

    def send_v(h):
        scatter(column_piece, vs, cv, 2 + h, h)

    def send_g(h):
        if h == 0:
            for k in range(2):
                l_g[k].wait()
        scatter(column_piece, gg, cg, 4 + h, h)

    def send_inner(h):
        scatter(column_piece, pin_s, ci, h, h)

    def send_fresh(k):
        fresh(fresh_columns, 10 + k, k)

    def factor_saved():
        l_f1.wait()
        for k in range(2):
            l_vs[k].wait()
            first_factor(vs, pin_s, k)

    def factor_fresh(k):
        l_vf[k].wait()
        first_factor(vf, pin_f, k)

    def fact_copy(by):
        return remote(
            f2_h, f2c.at[ks], nbs.at[by - 1], nbr.at[ks], {"seq": y * 4 + (x + by) % 4}
        )

    def tw_rows(c):
        return tw_h.at[at16(64 * y + 32 * c, 32), wide(512 * ks)]

    partner = {"mp": 1 - core}

    def lent():
        return (
            remote(tw_rows(1 - core), tws, nbs.at[3], nbr.at[2], partner),
            remote(up_h.at[ks], wup, nbs.at[4], nbr.at[3], partner),
            remote(dn_h.at[ks], wdn, nbs.at[5], nbr.at[4], partner),
        )

    def lend():
        @pl.when(home)
        def _():
            pltpu.make_async_copy(f2_h, f2c.at[ks], nbr.at[ks]).start()
            for by in range(1, 4):
                fact_copy(by).start()
            for copy in lent():
                copy.start()
            pltpu.make_async_copy(tw_rows(core), tws, nbr.at[2]).start()
            pltpu.make_async_copy(up_h.at[ks], wup, nbr.at[3]).start()
            pltpu.make_async_copy(dn_h.at[ks], wdn, nbr.at[4]).start()

    def block_diagonal(f2):
        rows, lanes = iota((512, 512), 0), iota((512, 512), 1)
        swap = jnp.where(lanes == (rows % 16) * 32 + rows // 16, 1.0, 0.0).astype(BF)
        spread = jnp.where(iota((32, 512), 1) // 16 == iota((32, 512), 0), 1.0, 0.0).astype(BF)
        ordered = nn(swap, f2).astype(BF)
        return jnp.where(rows % 16 == lanes % 16, nn(ordered, spread), 0.0).astype(BF)

    def near(ref, i):
        pltpu.make_async_copy(ref, ref, nbr.at[i]).wait()

    def fact_fresh():
        l_f2.wait()
        wmf[...] = block_diagonal(f2o[...])
        for k in range(2):
            l_tw[k].wait()

    def fact_saved():
        for h in range(2):
            near(f2c.at[h], h)
            wms[h] = block_diagonal(f2c[h])
        near(tws, 2)

    def small_copy(h, cc):
        return remote(
            sgp.at[h],
            sgr.at[x],
            sms.at[2 * h + cc],
            smr.at[x],
            {"seq": y * 4 + 2 * core + h, "mp": cc},
        )

    def twiddle_copy(h):
        return remote(
            twg.at[h],
            otw.at[:, wide(512 * ks)],
            sms.at[4 + h],
            smr.at[4 + ks],
            {"seq": y * 4 + 2 * core + h, "mp": kc},
        )

    def small_each(h, is_self, is_other):
        here = 2 * core + h == x
        for cc in range(2):
            same = jnp.logical_and(here, core == cc)

            if is_self:

                @pl.when(same)
                def _():
                    is_self(pltpu.make_async_copy(sgp.at[h], sgr.at[x], smr.at[x]))

            @pl.when(jnp.logical_not(same))
            def _():
                is_other(small_copy(h, cc))

        same = jnp.logical_and(here, home)

        if is_self:

            @pl.when(same)
            def _():
                is_self(
                    pltpu.make_async_copy(
                        twg.at[h], otw.at[:, wide(512 * ks)], smr.at[4 + ks]
                    )
                )

        @pl.when(jnp.logical_not(same))
        def _():
            is_other(twiddle_copy(h))

    def chunk(j):
        return pl.ds(pl.multiple_of(j * 512, 512), 512)

    def saved(h, mid=None, after=None):
        tw = tws[pl.ds(16 * h, 16), :].astype(F32)[None]
        arrived(ci.at[h], h)
        columns = (ci[h].astype(F32) * tw).astype(BF)
        twc[h] = columns
        mix[...] = nn(wms[h], columns.reshape(512, HALF)).astype(BF).reshape(32, 16, HALF)
        if mid:
            mid()
        arrived(cv.at[h], 2 + h)
        arrived(cg.at[h], 4 + h)
        if after:
            after()
        top = 512 * h

        def gated(r):
            blocks = pl.ds(r * 8, 8)
            values = cv[h, blocks].reshape(128, HALF).astype(F32)
            mixed = mix[blocks].reshape(128, HALF).astype(F32)
            return blocks, values, jax.nn.sigmoid(values), mixed

        def start(r, carry):
            blocks, values, gate, mixed = gated(r)
            hid[pl.ds(pl.multiple_of(top + r * 128, 128), 128), :] = (
                values + mixed * gate
            ).astype(BF)
            dh[pl.ds(pl.multiple_of(r * 128, 128), 128), :] = (
                cg[h, blocks].reshape(128, HALF).astype(F32)
            )
            return carry

        lax.fori_loop(0, 4, start, 0)
        if h == 0:
            near(wup, 3)
            near(wdn, 4)

        def step(j, carry):
            up_part = wup[:, chunk(j)]
            u = nn(hid[pl.ds(top, 512), :], up_part)
            back = nt(cg[h].reshape(512, HALF), wdn[chunk(j), :])
            square = u * u
            th = jnp.tanh(C0 * u * (1.0 + C1 * square))
            lift = 0.5 * (1.0 + th)
            act[j, pl.ds(top, 512), :] = (u * lift).astype(BF)
            slope = lift + (0.5 * C0) * u * (1.0 - th * th) * (1.0 + (3.0 * C1) * square)
            d_lift = (back * slope).astype(BF)
            dl[j, pl.ds(top, 512), :] = d_lift
            dh[...] += nt(d_lift, up_part)
            return carry

        lax.fori_loop(0, 4, step, 0)

        def end(r, carry):
            blocks, values, gate, mixed = gated(r)
            rs = pl.ds(pl.multiple_of(r * 128, 128), 128)
            d_hidden = dh[rs, :]
            dm[rs, :] = (d_hidden * gate).astype(BF)
            cdr[h, blocks] = (
                (d_hidden * (1.0 + mixed * gate * (1.0 - gate))).astype(BF).reshape(8, 16, HALF)
            )
            return carry

        lax.fori_loop(0, 4, end, 0)
        d_twisted = tn(wms[h], dm[...]).astype(BF).astype(F32).reshape(32, 16, HALF)
        cdi[h] = (d_twisted * tw).astype(BF)
        for a in range(2):
            scatter(position_piece, cdi, pdi, 6 + a, h)
            scatter(position_piece, cdr, pdr, 8 + a, h)
        twg[h] = jnp.sum(d_twisted * ci[h].astype(F32), axis=0)

        rows, lanes = iota((512, 512), 0), iota((512, 512), 1)
        product = nt(dm[...], twc[h].reshape(512, HALF))
        high, low = split(jnp.where(rows % 16 == lanes % 16, product, 0.0))
        packed = jnp.zeros((128, 128), F32)
        for group in range(4):
            gather = jnp.where(
                iota((512, 128), 1) == 32 * group + iota((512, 128), 0) // 16, 1.0, 0.0
            ).astype(BF)
            some = slice(128 * group, 128 * group + 128)
            packed = packed + nn(high[some], gather) + nn(low[some], gather)
        sgp[h] = packed
        small_each(h, lambda copy: copy.start(), lambda copy: copy.start())

    def second_fresh(k):
        arrived(cin_f.at[k], 10 + k)
        columns = (cin_f[k].astype(F32) * tw16[k].astype(F32)[None]).astype(BF)
        cmx_f[k] = nn(wmf[...], columns.reshape(512, HALF)).astype(BF).reshape(32, 16, HALF)
        fresh(fresh_positions, 12 + k, k)

    def gradients():
        def step_up(j, carry):
            total = tn(hid[...], dl[j]).astype(BF).reshape(4, 4, 32, 512)
            part[0, :, :, pl.ds(pl.multiple_of(j * 32, 32), 32), :] = total
            return carry

        lax.fori_loop(0, 4, step_up, 0)

        def step_down(j, carry):
            part[1, j] = tn(act[j], cg[...].reshape(1024, HALF)).astype(BF).reshape(4, 128, 512)
            return carry

        lax.fori_loop(0, 4, step_down, 0)

        for t in ORDER:
            core_copy(t).start()

    ORDER = (2, 1, 3, 0)

    def core_copy(t):
        return remote(
            part.at[1 - core, (y + t) % 4], mpb.at[t], mxs.at[t], mxr.at[t], partner
        )

    SLOTS = ((2, 0, 1), (1, 1, 1), (2, 1, 3), (3, 0, 3), (1, 0, 1), (3, 1, 3))

    def piece(by, h):
        return part.at[core, (y + by) % 4, pl.ds(2 * h, 2)]

    def rs_copy(slot):
        by, h, to = SLOTS[slot]
        return remote(
            piece(by, h),
            ra.at[slot],
            rss.at[slot],
            rsr.at[slot],
            {"seq": ((y + to) % 4) * 4 + x},
        )

    def both(t):
        core_copy(t).wait_recv()
        ref = part.at[core, (y + t) % 4]
        ref[...] = (ref[...].astype(F32) + mpb[t].astype(F32)).astype(BF)

    def core_sums():
        for t in ORDER:
            both(t)

    def rs_first():
        for slot in (0, 2, 1, 3):
            rs_copy(slot).start()

    def rs_second():
        for slot, after in ((4, 0), (5, 2)):
            by, h, to = SLOTS[slot]
            rs_copy(after).wait_recv()
            ref = piece(by, h)
            ref[...] = (ref[...].astype(F32) + ra[after].astype(F32)).astype(BF)
            rs_copy(slot).start()

    def spread_copy(xx):
        return remote(
            xsum.at[xx],
            wgr.at[core, ks],
            xss.at[xx],
            xsr.at[core, ks],
            {"seq": y * 4 + xx, "mp": kc},
        )

    def spread_each(xx, is_self, is_other):
        same = jnp.logical_and(x == xx, home)

        if is_self:

            @pl.when(same)
            def _():
                is_self(
                    pltpu.make_async_copy(xsum.at[xx], wgr.at[core, ks], xsr.at[core, ks])
                )

        @pl.when(jnp.logical_not(same))
        def _():
            is_other(spread_copy(xx))

    def rs_third():
        for h, left, right in ((0, 3, 4), (1, 1, 5)):
            for slot in (left, right):
                rs_copy(slot).wait_recv()
            xsum[pl.ds(2 * h, 2)] = (
                piece(0, h)[...].astype(F32) + ra[left].astype(F32) + ra[right].astype(F32)
            ).astype(BF)
            for xx in (2 * h, 2 * h + 1):
                spread_each(xx, lambda copy: copy.start(), lambda copy: copy.start())

    def act_copy(k):
        return remote(
            outf.at[k],
            oact.at[:, cols[k]],
            zs.at[k],
            zr.at[k],
            {"section": (sec + 1) % 4},
        )

    def grad_copy(k, a):
        half = pl.ds(256 * a, 256)
        return remote(
            dinp.at[k, half],
            ograd.at[half, cols[k]],
            zs.at[2 + 2 * a + k],
            zr.at[2 + 2 * a + k],
            {"section": (sec + 3) % 4},
        )

    def channel_fresh(k):
        def start(r, carry):
            rs = pl.ds(pl.multiple_of((r % 2) * 128, 128), 128)
            values = vf[k, r // 2, rs, :].astype(F32)
            mixed = pmx_f[k, r // 2, rs, :].astype(F32)
            hidden = (values + mixed * jax.nn.sigmoid(values)).astype(BF)
            pmx_f[k, r // 2, rs, :] = hidden
            dh[pl.ds(pl.multiple_of(r * 128, 128), 128), :] = hidden.astype(F32)
            return carry

        lax.fori_loop(0, 4, start, 0)

        def step(j, carry):
            u = nn(pmx_f[k].reshape(TOK, HALF), up[k, :, chunk(j)])
            th = jnp.tanh(C0 * u * (1.0 + C1 * (u * u)))
            dh[...] += nn((0.5 * u * (1.0 + th)).astype(BF), dn[k, chunk(j), :])
            return carry

        lax.fori_loop(0, 4, step, 0)
        outf[k] = dh[...].astype(BF)

    zero[...] = jnp.zeros_like(zero)

    def blank(dst, k, i):
        return pltpu.make_async_copy(zero, dst.at[:, cols[k]], osem.at[i])

    @pl.when(sec == 0)
    def _():
        for k in range(2):
            blank(oact, k, k).start()

    @pl.when(sec == NS - 1)
    def _():
        for k in range(2):
            blank(ograd, k, k).start()

    def mix_fresh(k):
        l_up[k].wait()
        l_dn[k].wait()
        arrived(pmx_f.at[k], 12 + k)
        channel_fresh(k)

        @pl.when(sec < NS - 1)
        def _():
            act_copy(k).start()

    def finish_saved():
        for a in range(2):
            arrived(pdr.at[:, a], 8 + a)
            arrived(pdi.at[:, a], 6 + a)
            for k in range(2):
                dinp[k, pl.ds(256 * a, 256), :] = (
                    pdr[k, a].astype(F32) + tn(f1[a], pdi[k, a])
                ).astype(BF)

            @pl.when(sec > 0)
            def _():
                for k in range(2):
                    grad_copy(k, a).start()

    pl.semaphore_wait(barrier, 2 * NQ + 1)

    lend()
    factor_saved()
    send_inner(0)
    send_v(0)
    send_g(0)
    send_inner(1)
    send_v(1)
    send_g(1)
    factor_fresh(0)
    send_fresh(0)
    factor_fresh(1)
    send_fresh(1)
    fact_fresh()
    fact_saved()
    saved(0)
    second_fresh(0)
    second_fresh(1)
    saved(1)
    gradients()
    core_sums()
    rs_first()
    mix_fresh(0)
    finish_saved()
    rs_second()
    mix_fresh(1)
    rs_third()

    for a in range(2):
        fg[a] = nt(pdi[0, a], vs[0, a]) + nt(pdi[1, a], vs[1, a])
    first_copy = remote(fg, fg_r, mxs.at[4], mxr.at[4], partner)
    first_copy.start()

    def store(src, dst, i):
        copy = pltpu.make_async_copy(src, dst, osem.at[i])
        copy.start()
        return copy

    for k in range(4):
        pltpu.make_async_copy(sgr.at[k], sgr.at[k], smr.at[k]).wait()
    packed = (sgr[0] + sgr[1]) + (sgr[2] + sgr[3])
    high, low = split(packed)
    for group in range(4):
        pick = jnp.where(iota((128, 32), 0) == 32 * group + iota((128, 32), 1), 1.0, 0.0).astype(
            BF
        )
        sg[pl.ds(128 * group, 128), :] = nn(high, pick) + nn(low, pick)
    rows, lanes = iota((512, 512), 0), iota((512, 512), 1)
    back_swap = jnp.where(lanes == (rows % 32) * 16 + rows // 32, 1.0, 0.0).astype(BF)
    high, low = split(sg[...])
    sgo[...] = nn(back_swap, high) + nn(back_swap, low)
    stores = [store(sgo, osecond, 2)]
    first_copy.wait()
    fg[...] += fg_r[...]
    stores.append(store(fg, ofirst, 3))
    for slot in range(2):
        for kind in range(2):
            pltpu.make_async_copy(
                wgr.at[kind, slot], wgr.at[kind, slot], xsr.at[kind, slot]
            ).wait()
        for j in range(4):
            upo[slot, :, pl.ds(512 * j, 512)] = wgr[0, slot, pl.ds(32 * j, 32), :].astype(F32)
        dno[slot] = wgr[1, slot].astype(F32)
        stores.append(store(upo.at[slot], oup.at[slot], 4 + slot))
        stores.append(store(dno.at[slot], odn.at[slot], 6 + slot))

    sent = ((pin_s, 0, 0), (vs, 2, 0), (gg, 4, 0), (cdi, 6, 2), (cdr, 8, 2), (pin_f, 10, 0), (cmx_f, 12, 1))
    for src, i, kind in sent:
        for k in range(2):
            if kind == 0:
                most, rest = src.at[k, :, pl.ds(0, 240), :], src.at[k, :, pl.ds(0, 16), :]
            elif kind == 1:
                most, rest = src.at[k, pl.ds(0, 30)], None
            else:
                most, rest = src.at[:, pl.ds(0, 15)], src.at[:, pl.ds(0, 1)]
            pltpu.make_async_copy(most, most, a2s.at[i + k]).wait()
            if i < 10:

                @pl.when(away)
                def _():
                    pltpu.make_async_copy(rest, rest, a2s.at[i + k]).wait()

    @pl.when(home)
    def _():
        for by in range(1, 4):
            fact_copy(by).wait_send()
        for copy in lent():
            copy.wait_send()

    for h in range(2):
        small_each(h, None, lambda copy: copy.wait_send())
    for slot in range(2):
        otw_part = otw.at[:, cols[slot]]
        pltpu.make_async_copy(otw_part, otw_part, smr.at[4 + slot]).wait()
    for t in range(4):
        core_copy(t).wait_send()
    for slot in range(6):
        rs_copy(slot).wait_send()
    for xx in range(4):
        spread_each(xx, None, lambda copy: copy.wait_send())

    @pl.when(sec < NS - 1)
    def _():
        for k in range(2):
            act_copy(k).wait_send()
            for a in range(2):
                grad_copy(k, a).wait_recv()

    @pl.when(sec > 0)
    def _():
        for k in range(2):
            act_copy(k).wait_recv()
            for a in range(2):
                grad_copy(k, a).wait_send()

    @pl.when(sec == 0)
    def _():
        for k in range(2):
            blank(oact, k, k).wait()

    @pl.when(sec == NS - 1)
    def _():
        for k in range(2):
            blank(ograd, k, k).wait()

    for copy in stores:
        copy.wait()


def hand_on(*refs):
    count = (len(refs) - 1) // 3
    sems = refs[-1]
    pieces = []
    for i in range(count):
        size = refs[i].shape[0]
        cut = 128 if size == TOK else 1 if size == GRP else size
        pieces += [(i, pl.ds(start, cut)) for start in range(0, size, cut)]
    into, out = [], []
    for n, (i, at) in enumerate(pieces):
        held = refs[2 * count + i].at[at]
        into.append(pltpu.make_async_copy(refs[i].at[at], held, sems.at[0, n]))
        out.append(pltpu.make_async_copy(held, refs[count + i].at[at], sems.at[1, n]))
    for copy in into:
        copy.start()
    for first, second in zip(into, out):
        first.wait()
        second.start()
    for copy in out:
        copy.wait()


def body(fresh, saved, cotangent, factor_one, twiddle, factor_two, up_weight, down_weight):
    any_space = pl.BlockSpec(memory_space=pl.ANY)
    position = pltpu.VMEM((2, 2, 256, HALF), BF)
    column = pltpu.VMEM((2, 32, 16, HALF), BF)
    rows = pltpu.VMEM((2, TOK, HALF), BF)
    square = pltpu.VMEM((512, 512), BF)
    fact = pltpu.VMEM((512, 32), BF)
    dma = pltpu.SemaphoreType.DMA
    shapes = (
        jax.ShapeDtypeStruct((TOK, 1024), BF),
        jax.ShapeDtypeStruct((TOK, 1024), BF),
        jax.ShapeDtypeStruct((2, 32, FB), F32),
        jax.ShapeDtypeStruct((2, 128, 512), F32),
        jax.ShapeDtypeStruct((16, 1024), F32),
        jax.ShapeDtypeStruct((2, 256, 256), F32),
        jax.ShapeDtypeStruct((512, 32), F32),
    )
    outs = pl.pallas_call(
        kernel,
        out_shape=shapes,
        in_specs=[any_space] * 8,
        out_specs=(any_space,) * 7,
        scratch_shapes=[
            position, position, position,
            pltpu.VMEM((2, 256, 256), BF),
            pltpu.VMEM((2, 16, HALF), BF),
            pltpu.VMEM((32, HALF), BF),
            fact,
            pltpu.VMEM((2, 512, 32), BF),
            pltpu.VMEM((2, 512, FB), BF),
            pltpu.VMEM((2, FB, 512), BF),
            pltpu.VMEM((512, FB), BF),
            pltpu.VMEM((FB, 512), BF),
            square,
            pltpu.VMEM((2, 512, 512), BF),
            position, position, position, position, position,
            column, column, column, column, column, column, column,
            column,
            pltpu.VMEM((32, 16, HALF), BF),
            square,
            pltpu.VMEM((2 * TOK, HALF), BF),
            pltpu.VMEM((4, 2 * TOK, 512), BF),
            pltpu.VMEM((4, 2 * TOK, 512), BF),
            pltpu.VMEM((TOK, HALF), F32),
            pltpu.VMEM((2, 4, 4, 128, 512), BF),
            pltpu.VMEM((4, 4, 128, 512), BF),
            pltpu.VMEM((6, 2, 128, 512), BF),
            pltpu.VMEM((4, 128, 512), BF),
            pltpu.VMEM((2, 2, 128, 512), BF),
            pltpu.VMEM((2, 256, 256), F32),
            pltpu.VMEM((2, 256, 256), F32),
            pltpu.VMEM((2, 128, 128), F32),
            pltpu.VMEM((4, 128, 128), F32),
            pltpu.VMEM((512, 32), F32),
            rows, rows,
            pltpu.VMEM((TOK, HALF), BF),
            pltpu.VMEM((2, 32, FB), F32),
            pltpu.VMEM((2, 128, 512), F32),
            pltpu.VMEM((2, 16, HALF), F32),
            pltpu.VMEM((512, 32), F32),
            dma((14,)), dma((14,)), dma((14,)), dma((6,)), dma((5,)), dma((6,)), dma((6,)),
            dma((5,)), dma((5,)), dma((4,)), dma((2, 2)), dma((6,)), dma((6,)),
            dma((6,)), dma((6,)), dma((8,)),
        ],
        compiler_params=pltpu.CompilerParams(
            collective_id=0, has_side_effects=True, vmem_limit_bytes=63 * 1024 * 1024
        ),
    )(
        fresh.reshape(2, 256, 1024), saved.reshape(2, 256, 1024), cotangent.reshape(2, 256, 1024),
        factor_one[0], twiddle[0], factor_two[0].reshape(512, 32), up_weight[0], down_weight[0],
    )
    act, grad, up_grad, down_grad, twiddle_grad, first_grad, second_grad = pl.pallas_call(
        hand_on,
        out_shape=shapes,
        in_specs=[any_space] * 7,
        out_specs=(any_space,) * 7,
        scratch_shapes=[pltpu.VMEM(part.shape, part.dtype) for part in shapes] + [dma((2, 19))],
    )(*outs)
    return (
        act[None],
        grad[None],
        up_grad[None],
        down_grad[None],
        twiddle_grad[None],
        first_grad[None],
        second_grad.reshape(1, 16, 32, 32),
    )


def solution(mesh):
    return jax.shard_map(
        body,
        mesh=mesh,
        in_specs=(
            P("section", "seq", "mp"),
            P("section", "seq", "mp"),
            P("section", "seq", "mp"),
            P("section", "seq", None, None),
            P("section", None, "mp"),
            P("section", "seq", None, None),
            P("section", "mp", None, None),
            P("section", "mp", None, None),
        ),
        out_specs=(
            P("section", "seq", "mp"),
            P("section", "seq", "mp"),
            P("section", "mp", "seq", None),
            P("section", "mp", "seq", None),
            P("section", "seq", "mp"),
            P("section", "seq", None, None),
            P("section", "seq", None, None),
        ),
        check_vma=False,
    )
```
